128 devices in a mesh: patch: 64 (over z_lo, y, x, core), frame: 2 (over z_hi).
Axes of the slice: x: 4, y: 4, z: 4 (z_hi: 2, z_lo: 2; z = z_hi * 2 + z_lo), core: 2. Of those that a mesh axis runs over, the one named last changes fastest.
Arguments:
- basis: bfloat16 [3, 16384, 1024], P(None, 'patch'), may hold values from -0.5 to 0.5
- latents: bfloat16 [1024, 1024], P('frame', 'patch'), may hold values from -2 to 2
- rest_pos: float32 [3, 16384], P(None, 'patch'), may hold values from -3 to 3
- triangles: int32 [3, 32768], P(None, 'patch'), may hold values from 0 to 511
- hinges: int32 [4, 24576], P(None, 'patch'), may hold values from 0 to 511
- rest_sq: float32 [3, 32768], P(None, 'patch'), may hold values from 0.5 to 3
- bend_rest: float32 [3, 24576], P(None, 'patch'), may hold values from -5 to 5
- masses: float32 [16384], P('patch'), may hold values from 0.5 to 2
- send_rows: int32 [2, 8192], P(None, 'patch'), may hold values from 0 to 255, as said below
Outputs:
- basis_grad: float32 [3, 16384, 1024], P(None, ('patch', 'frame'))
- latent_grad: float32 [1024, 1024], P('frame', 'patch')
The draws below stay inside these ranges and needn't reach their ends.
Inputs may be any that keep to these rules, and one draw needn't show every extreme that they name: `send_rows`: within one patch's columns the 256 entries of both rows are distinct own vertex numbers.
All inputs are finite; a program needn't handle non-finite values.
Results may differ from the reference program's by a relative error of at most 0.006.
Values may be sent and summed in bfloat16 or wider, within the bound.
No kernel may reach another device: no remote copies, remote signals or barrier semaphores. Data moves between devices by JAX's collectives and lax.ppermute only.
A program may use at most 64 MiB of HBM per device.

```python
import math
import jax
import jax.numpy as jnp
from jax import lax

LATENT = 1024
VDEV = 256
FR_DEV = 512
HALO = 128
VERTS = 16384
FRAMES = 1024
TRIS = 32768
HINGES = 24576
N_PATCH = 64
N_FRAME = 2


def draw_send_rows(key, part):
    keys = jax.random.split(jax.random.fold_in(key, 17), N_PATCH)

    def one_patch(patch_key):
        shuffled = jax.random.permutation(patch_key, VDEV)
        return shuffled[:2 * HALO].reshape(2, HALO)
    chosen = jax.vmap(one_patch)(keys)
    return jnp.transpose(chosen, (1, 0, 2)).reshape(2, N_PATCH * HALO).astype(jnp.int32)


def plant(values, rng, low, high):
    longest = values.shape.index(max(values.shape))
    spots = []
    for shift in (0, 1):
        where = [jax.random.randint(jax.random.fold_in(rng, axis), (), 0, length) for axis, length in enumerate(values.shape)]
        where[longest] = (where[longest] + shift) % values.shape[longest]
        spots.append(tuple(where))
    return values.at[spots[0]].set(low).at[spots[1]].set(high)


def spiked(entries, own_key, source, target, shards_of, factor):
    def block_of(position):
        return (jnp.arange(entries.shape[position]) // (entries.shape[position] // shards_of)).reshape((-1,) + (1,) * (entries.ndim - 1 - position))

    one_side = jax.random.permutation(own_key, shards_of)[block_of(target)]
    second = (block_of(target) + shards_of // 2) % shards_of
    return jnp.where((block_of(source) == one_side) | (block_of(source) == second), factor * entries, entries)


def shard_levels(key, dims, pieces, least, largest):
    loudness, own = 1.0, jax.random.fold_in(key, 6)
    for axis_at, blocks in pieces:
        steps = jnp.exp(jax.random.uniform(jax.random.fold_in(own, axis_at), (blocks,), jnp.float32, least / len(pieces), largest / len(pieces)))
        loudness = loudness * jnp.repeat(steps, dims[axis_at] // blocks).reshape([-1 if axis == axis_at else 1 for axis in range(len(dims))])
    return loudness


def centred(key, extent, width, most, cuts=(), held_as=jnp.bfloat16):
    result = jax.random.normal(key, extent, jnp.float32) * width
    if len(cuts) > 0:
        result = shard_levels(key, extent, cuts, -0.22, 0.18) * result
    return jnp.clip(result, min=-most, max=most).astype(held_as)


def heavy_noise(key, extent, deviation, reach, cuts, heavy, kind=jnp.bfloat16):
    values = deviation * jax.random.normal(key, extent, jnp.float32)
    if cuts:
        values = values * shard_levels(key, extent, cuts, -0.22, 0.18)
    return jnp.clip(spiked(values, jax.random.fold_in(key, 3), *heavy), -reach, reach).astype(kind)


def setup_inputs(seed: int = 0) -> dict:
    splits = jax.random.split(jax.random.key(seed), 10)
    basis = heavy_noise(splits[0], (3, VERTS, LATENT), LATENT ** -0.5, 0.5, ((1, 64),), (1, 2, 64, 4.0))
    latents = centred(splits[1], (FRAMES, LATENT), 0.3, 2.0, ((0, 2), (1, 64)))
    rest_pos = centred(splits[2], (3, VERTS), 0.5, 3.0, ((1, 64),), jnp.float32)
    triangles = plant(jax.random.randint(splits[3], (3, TRIS), 0, VDEV + 2 * HALO), jax.random.fold_in(splits[3], 1), 0, (VDEV + 2 * HALO) - 1).astype(jnp.int32)
    hinges = plant(jax.random.randint(splits[4], (4, HINGES), 0, VDEV + 2 * HALO), jax.random.fold_in(splits[4], 1), 0, (VDEV + 2 * HALO) - 1).astype(jnp.int32)
    rest_sq = jnp.clip(jnp.exp(math.log(3.0) - 1.7917595 * jax.random.uniform(splits[5], (3, TRIS), jnp.float32) ** shard_levels(splits[5], (3, TRIS), ((1, 64),), -0.2, 0.2)), 0.5, 3.0)
    bend_rest = centred(splits[6], (3, HINGES), 1.0, 5.0, ((1, 64),), jnp.float32)
    masses = jnp.clip(jnp.exp(math.log(2.0) - 1.3862944 * jax.random.uniform(splits[7], (VERTS,), jnp.float32) ** shard_levels(splits[7], (VERTS,), ((0, 64),), -0.2, 0.2)), 0.5, 2.0)
    send_rows = draw_send_rows(jax.random.fold_in(splits[9], 71), 0)
    return dict(basis=basis, latents=latents, rest_pos=rest_pos, triangles=triangles, hinges=hinges, rest_sq=rest_sq, bend_rest=bend_rest, masses=masses, send_rows=send_rows)


MEMBRANE = 5.0
BENDING = 5.0
GRAVITY = 40.0

def elastic(points, corners, hinge_ids, rest_sq, bend_rest):
    point_one = points[:, :, corners[0]]
    point_two = points[:, :, corners[1]]
    point_three = points[:, :, corners[2]]
    edge_list = (point_two - point_one, point_three - point_two, point_one - point_three)
    membrane = jnp.float32(0.0)
    for corner_slot in range(3):
        strain = lax.optimization_barrier(jnp.sum(edge_list[corner_slot] * edge_list[corner_slot], axis=1)) - rest_sq[corner_slot]
        membrane = membrane + jnp.sum(strain * strain)
    bending = points[:, :, hinge_ids[2]] + points[:, :, hinge_ids[3]] - points[:, :, hinge_ids[0]] - points[:, :, hinge_ids[1]] - bend_rest
    return MEMBRANE * membrane + BENDING * jnp.sum(bending * bending)

def extend_ids(local_ids, send_rows):
    row_count = local_ids.shape[0]
    grouped = local_ids.reshape(row_count, N_PATCH, -1)
    senders = send_rows.reshape(2, N_PATCH, HALO)
    device_ids = jnp.arange(N_PATCH, dtype=jnp.int32)[None, :, None]
    previous = (device_ids + N_PATCH - 1) % N_PATCH
    following = (device_ids + 1) % N_PATCH
    from_prev = senders[1][previous, jnp.clip(grouped - VDEV, 0, HALO - 1)] + previous * VDEV
    from_next = senders[0][following, jnp.clip(grouped - VDEV - HALO, 0, HALO - 1)] + following * VDEV
    global_ids = jnp.where(grouped < VDEV, grouped + device_ids * VDEV, jnp.where(grouped < VDEV + HALO, from_prev, from_next))
    return global_ids.reshape(row_count, -1).astype(jnp.int32)

def reference(basis, latents, rest_pos, triangles, hinges, rest_sq, bend_rest, masses, send_rows):
    corners = extend_ids(triangles, send_rows)
    hinge_ids = extend_ids(hinges, send_rows)
    flat_basis = basis.reshape(3 * VERTS, LATENT)
    decoded = jnp.dot(latents, flat_basis.T, preferred_element_type=jnp.float32)
    positions = rest_pos[None] + decoded.reshape(FRAMES, 3, VERTS)
    frame_block = min(32, FRAMES)
    stacked = positions.reshape(FRAMES // frame_block, frame_block, 3, VERTS)
    force_fn = jax.grad(elastic)
    grads = lax.map(lambda frames_block: force_fn(frames_block, corners, hinge_ids, rest_sq, bend_rest), stacked)
    grads = grads.reshape(FRAMES, 3, VERTS)
    grads = grads.at[:, 2, :].add(GRAVITY * masses)
    adjoint = (grads / FRAMES).astype(jnp.bfloat16)
    flat_adjoint = adjoint.reshape(FRAMES, 3 * VERTS)
    latent_grad = jnp.dot(flat_adjoint, flat_basis, preferred_element_type=jnp.float32)
    total = jnp.zeros((3 * VERTS, LATENT), jnp.float32)
    for half_index in range(N_FRAME):
        lower = half_index * FR_DEV
        partial_sum = jnp.dot(flat_adjoint[lower:lower + FR_DEV].T, latents[lower:lower + FR_DEV], preferred_element_type=jnp.float32)
        rounded = lax.optimization_barrier(partial_sum.astype(jnp.bfloat16))
        total = total + rounded.astype(jnp.float32)
    return (total.reshape(3, VERTS, LATENT), latent_grad)
```

```python
import functools

import jax
import jax.numpy as jnp
from jax import lax
from jax.experimental import pallas as pl
from jax.experimental.pallas import tpu as pltpu
from jax.sharding import PartitionSpec as P

MEMBRANE = 5.0
BENDING = 5.0
GRAVITY = 40.0
BF = jnp.bfloat16
F32 = jnp.float32
NN = (((1,), (0,)), ((), ()))
TN = (((0,), (0,)), ((), ()))
NT = (((1,), (1,)), ((), ()))
PARAMS = pltpu.CompilerParams(vmem_limit_bytes=48 * 1024 * 1024)


def dot(a, b, dims=NN):
    return lax.dot_general(a, b, dims, preferred_element_type=F32)


def exact_dot(a, b):
    total = None
    for _ in range(3):
        part = b.astype(BF)
        b = b - part.astype(F32)
        term = dot(a, part)
        total = term if total is None else total + term
    return total


def one_hot(rows, ids):
    return (lax.broadcasted_iota(jnp.int32, (rows, ids.shape[1]), 0) == ids).astype(F32)


def pick_kernel(send_ref, basis_ref, prev_ref, next_ref):
    own, halo = basis_ref.shape[1], send_ref.shape[1]
    for row, out in ((0, prev_ref), (1, next_ref)):
        sel = one_hot(own, send_ref[row : row + 1, :]).astype(BF)
        for c in range(3):
            out[c * halo : (c + 1) * halo, :] = dot(sel, basis_ref[c], TN).astype(BF)


def incidence_kernel(tri_ref, hin_ref, d_ref, dt_ref):
    ext = dt_ref.shape[0]
    t = tri_ref.shape[1]
    a, b, c = (one_hot(ext, tri_ref[i : i + 1, :]) for i in range(3))
    for at, part in ((0, b - a), (t, c - b)):
        dt_ref[:, at : at + t] = part.astype(BF)
        d_ref[at : at + t, :] = part.T.astype(BF)
    a, b, c, d = (one_hot(ext, hin_ref[i : i + 1, :]) for i in range(4))
    part = c + d - a - b
    dt_ref[:, 2 * t :] = part.astype(BF)
    d_ref[2 * t :, :] = part.T.astype(BF)


def elastic_kernel(
    frames, own_n, halo,
    lat_ref, own_ref, prv_ref, nxt_ref, d_ref, dt_ref, off_ref, sq_ref, grav_ref,
    f_own_ref, f_prv_ref, f_nxt_ref, lg_ref,
):
    t = sq_ref.shape[1]
    lat = lat_ref[...]
    x_own = dot(own_ref[...], lat).astype(BF)
    x_prv = dot(prv_ref[...], lat).astype(BF)
    x_nxt = dot(nxt_ref[...], lat).astype(BF)
    d = d_ref[...]
    edges = []
    for c in range(3):
        x = jnp.concatenate(
            [
                x_own[c * own_n : (c + 1) * own_n],
                x_prv[c * halo : (c + 1) * halo],
                x_nxt[c * halo : (c + 1) * halo],
            ],
            axis=0,
        )
        edges.append(dot(d, x) + off_ref[c])
    e1 = [e[:t] for e in edges]
    e2 = [e[t : 2 * t] for e in edges]
    q1 = e1[0] * e1[0] + e1[1] * e1[1] + e1[2] * e1[2]
    q2 = e2[0] * e2[0] + e2[1] * e2[1] + e2[2] * e2[2]
    e3 = [u + v for u, v in zip(e1, e2)]
    q3 = e3[0] * e3[0] + e3[1] * e3[1] + e3[2] * e3[2]
    scale = 4.0 * MEMBRANE / frames
    s1, s2, s3 = (scale * (q - sq_ref[i]) for i, q in enumerate((q1, q2, q3)))
    dt = dt_ref[...]
    for c in range(3):
        third = s3 * e3[c]
        g = jnp.concatenate(
            [
                (s1 * e1[c] + third).astype(BF),
                (s2 * e2[c] + third).astype(BF),
                (edges[c][2 * t :] * (2.0 * BENDING / frames)).astype(BF),
            ],
            axis=0,
        )
        f = dot(dt, g)
        f_own = f[:own_n]
        if c == 2:
            f_own = f_own + grav_ref[...]
        f_own_ref[c * own_n : (c + 1) * own_n, :] = f_own
        f_prv_ref[c * halo : (c + 1) * halo, :] = f[own_n : own_n + halo].astype(BF)
        f_nxt_ref[c * halo : (c + 1) * halo, :] = f[own_n + halo :].astype(BF)
    lg = dot(own_ref[...], f_own_ref[...].astype(BF), TN)
    lg = lg + dot(prv_ref[...], f_prv_ref[...], TN)
    lg = lg + dot(nxt_ref[...], f_nxt_ref[...], TN)
    lg_ref[...] = lg.astype(BF)


def adjoint_kernel(send_ref, f_own_ref, back_prv_ref, back_nxt_ref, adj_ref):
    halo = send_ref.shape[1]
    own = f_own_ref.shape[0] // 3
    half = own // 2
    to_prev = one_hot(own, send_ref[0:1, :]).astype(BF)
    to_next = one_hot(own, send_ref[1:2, :]).astype(BF)
    for c in range(3):
        rows = slice(c * halo, (c + 1) * halo)
        total = f_own_ref[c * own : (c + 1) * own, :]
        total = total + dot(to_prev, back_prv_ref[rows, :]) + dot(to_next, back_nxt_ref[rows, :])
        total = total.astype(BF)
        for h in range(2):
            adj_ref[h, c * half : (c + 1) * half, :] = total[h * half : (h + 1) * half]


def basis_grad_kernel(mine_ref, other_ref, lat_mine_ref, lat_other_ref, out_ref):
    one = dot(mine_ref[...], lat_mine_ref[...], NT).astype(BF).astype(F32)
    two = dot(other_ref[...], lat_other_ref[...], NT).astype(BF).astype(F32)
    out_ref[...] = one + two


def call(kernel, outs, *args):
    return pl.pallas_call(
        kernel,
        out_shape=[jax.ShapeDtypeStruct(s, d) for s, d in outs],
        compiler_params=PARAMS,
    )(*args)


def local(basis, latents, rest_pos, triangles, hinges, rest_sq, bend_rest, masses, send_rows):
    own = basis.shape[1]
    width = basis.shape[2]
    frames = latents.shape[0]
    each = latents.shape[1]
    halo = send_rows.shape[1]
    tris = triangles.shape[1]
    hings = hinges.shape[1]
    ext = own + 2 * halo
    patches = lax.axis_size("patch")
    total_frames = frames * lax.axis_size("frame")
    chips = patches // 2
    onward = [(i, (i + 1) % patches) for i in range(patches)]
    backward = [((i + 1) % patches, i) for i in range(patches)]
    sibling = [(i, i ^ 1) for i in range(patches)]
    partner = [(0, 1), (1, 0)]
    same_core = [[2 * i + c for i in range(chips)] for c in range(2)]
    core = lax.axis_index("patch") % 2
    half_index = lax.axis_index("frame")

    def exchange(tiles):
        return lax.all_to_all(tiles, "patch", 0, 0, tiled=True, axis_index_groups=same_core)

    def interleaved(mine, other):
        both = jnp.where(
            core == 0, jnp.stack([mine, other], axis=1), jnp.stack([other, mine], axis=1)
        )
        return both.reshape(width, frames)

    shard = latents.T
    lat_core = exchange(jnp.broadcast_to(shard[None], (chips, each, frames)))
    rows_prev, rows_next = call(
        pick_kernel, [((3 * halo, width), BF)] * 2, send_rows, basis
    )
    halo_prv = lax.ppermute(rows_next, "patch", onward)
    halo_nxt = lax.ppermute(rows_prev, "patch", backward)
    d, dt = call(
        incidence_kernel,
        [((2 * tris + hings, ext), BF), ((ext, 2 * tris + hings), BF)],
        triangles,
        hinges,
    )
    sel = send_rows[:, :, None] == lax.broadcasted_iota(jnp.int32, (2, halo, own), 2)
    sent_rest = jnp.sum(jnp.where(sel[:, None], rest_pos[None, :, None, :], 0.0), axis=3)
    rest_prv = lax.ppermute(sent_rest[1], "patch", onward)
    rest_nxt = lax.ppermute(sent_rest[0], "patch", backward)
    rest_ext = jnp.concatenate([rest_pos, rest_prv, rest_nxt], axis=1)

    def offsets_kernel(d_ref, rest_ref, bend_ref, off_ref):
        off_ref[...] = exact_dot(d_ref[...], rest_ref[...]) - bend_ref[...]

    rest_cols = jnp.pad(rest_ext.T, ((0, 0), (0, 125)))
    bend_cols = jnp.pad(bend_rest.T, ((2 * tris, 0), (0, 125)))
    [offs] = call(offsets_kernel, [((2 * tris + hings, 128), F32)], d, rest_cols, bend_cols)
    offsets = offs[:, :3].T[:, :, None]
    sq_cols = rest_sq[:, :, None]
    gravity = (masses * (GRAVITY / total_frames))[:, None]

    lat_sib = lax.ppermute(lat_core, "patch", sibling)
    lat_all = interleaved(lat_core, lat_sib)

    step = min(frames, 256)
    full = lambda shape: pl.BlockSpec(shape, lambda i: (0,) * len(shape))
    cols = lambda rows: pl.BlockSpec((rows, step), lambda i: (0, i))
    f_own, f_prv, f_nxt, lg = pl.pallas_call(
        functools.partial(elastic_kernel, total_frames, own, halo),
        grid=(frames // step,),
        in_specs=[
            cols(width),
            full((3 * own, width)),
            full((3 * halo, width)),
            full((3 * halo, width)),
            full((2 * tris + hings, ext)),
            full((ext, 2 * tris + hings)),
            full((3, 2 * tris + hings, 1)),
            full((3, tris, 1)),
            full((own, 1)),
        ],
        out_specs=[cols(3 * own), cols(3 * halo), cols(3 * halo), cols(width)],
        out_shape=[
            jax.ShapeDtypeStruct((3 * own, frames), F32),
            jax.ShapeDtypeStruct((3 * halo, frames), BF),
            jax.ShapeDtypeStruct((3 * halo, frames), BF),
            jax.ShapeDtypeStruct((width, frames), BF),
        ],
        compiler_params=PARAMS,
    )(lat_all, basis.reshape(3 * own, width), halo_prv, halo_nxt, d, dt, offsets, sq_cols, gravity)

    back_nxt = lax.ppermute(f_prv, "patch", backward)
    back_prv = lax.ppermute(f_nxt, "patch", onward)

    lg = lg.reshape(chips, 2, each, frames)
    keep = jnp.where(core == 0, lg[:, 0], lg[:, 1])
    give = jnp.where(core == 0, lg[:, 1], lg[:, 0])
    got = lax.ppermute(give, "patch", sibling)
    pair = (keep.astype(F32) + got.astype(F32)).astype(BF)
    shares = exchange(pair)
    latent_grad = jnp.sum(shares.astype(F32), axis=0).T

    far_core = lax.ppermute(lat_core, "frame", partner)
    far_sib = lax.ppermute(far_core, "patch", sibling)
    lat_far = interleaved(far_core, far_sib)

    half = own // 2
    [adj] = call(
        adjoint_kernel, [((2, 3 * half, frames), BF)], send_rows, f_own, back_prv, back_nxt
    )
    mine = jnp.where(half_index == 0, adj[0], adj[1])
    other = jnp.where(half_index == 0, adj[1], adj[0])
    received = lax.ppermute(other, "frame", partner)
    [basis_grad] = call(
        basis_grad_kernel, [((3 * half, width), F32)], mine, received, lat_all, lat_far
    )
    return basis_grad.reshape(3, half, width), latent_grad


def solution(mesh):
    return jax.shard_map(
        local,
        mesh=mesh,
        in_specs=(
            P(None, "patch", None),
            P("frame", "patch"),
            P(None, "patch"),
            P(None, "patch"),
            P(None, "patch"),
            P(None, "patch"),
            P(None, "patch"),
            P("patch"),
            P(None, "patch"),
        ),
        out_specs=(P(None, ("patch", "frame"), None), P("frame", "patch")),
        check_vma=False,
    )
```

```python
import functools

import jax
import jax.numpy as jnp
from jax import lax
from jax.experimental import pallas as pl
from jax.experimental.pallas import tpu as pltpu
from jax.sharding import PartitionSpec as P

MEMBRANE = 5.0
BENDING = 5.0
GRAVITY = 40.0
BF = jnp.bfloat16
F32 = jnp.float32
NN = (((1,), (0,)), ((), ()))
TN = (((0,), (0,)), ((), ()))
NT = (((1,), (1,)), ((), ()))
PARAMS = pltpu.CompilerParams(vmem_limit_bytes=48 * 1024 * 1024)


def dot(a, b, dims=NN):
    return lax.dot_general(a, b, dims, preferred_element_type=F32)


def exact_dot(a, b):
    total = None
    for _ in range(3):
        part = b.astype(BF)
        b = b - part.astype(F32)
        term = dot(a, part)
        total = term if total is None else total + term
    return total


def one_hot(rows, ids):
    return (lax.broadcasted_iota(jnp.int32, (rows, ids.shape[1]), 0) == ids).astype(F32)


def column_block(rows):
    n, width = rows.shape
    return jnp.concatenate([rows, jnp.zeros((128 - n, width), F32)], axis=0).T


def interleave(core, mine_ref, other_ref, out_ref):
    chips, each, _ = mine_ref.shape
    for i in range(chips):
        out_ref[pl.ds(pl.multiple_of((2 * i + core) * each, each), each), :] = mine_ref[i]
        out_ref[pl.ds(pl.multiple_of((2 * i + 1 - core) * each, each), each), :] = other_ref[i]


def pick_kernel(send_ref, basis_ref, rest_ref, prev_ref, next_ref):
    own, halo = basis_ref.shape[1], send_ref.shape[1]
    rest = rest_ref[...]
    parts = []
    for _ in range(3):
        part = rest.astype(BF)
        rest = rest - part.astype(F32)
        parts.append(part.astype(F32))
    parts.append(jnp.zeros((7, own), F32))
    parts = jnp.concatenate(parts, axis=0).astype(BF)
    for row, out in ((0, prev_ref), (1, next_ref)):
        sel = one_hot(own, send_ref[row : row + 1, :]).astype(BF)
        for c in range(3):
            out[c * halo : (c + 1) * halo, :] = dot(sel, basis_ref[c], TN).astype(BF)
        out[3 * halo :, :] = jnp.zeros((out.shape[0] - 3 * halo, out.shape[1]), BF)
        out[3 * halo :, :halo] = dot(parts, sel).astype(BF)


def incidence_kernel(tri_ref, hin_ref, d_ref, dt_ref, b_ref, bt_ref, lap_ref):
    ext = dt_ref.shape[0]
    t = tri_ref.shape[1]
    a, b, c = (one_hot(ext, tri_ref[i : i + 1, :]) for i in range(3))
    for at, part in ((0, b - a), (t, c - b)):
        dt_ref[:, at : at + t] = part.astype(BF)
        d_ref[at : at + t, :] = part.T.astype(BF)
    a, b, c, d = (one_hot(ext, hin_ref[i : i + 1, :]) for i in range(4))
    part = c + d - a - b
    bt_ref[...] = part.astype(BF)
    b_ref[...] = part.T.astype(BF)
    lap_ref[...] = dot(bt_ref[...], b_ref[...]).astype(BF)


def constants_kernel(
    frames,
    rest_ref, mass_ref, prv_ref, nxt_ref, bend_ref, sq_ref, d_ref, b_ref, bt_ref, own_ref,
    edge_ref, vert_ref, sqc_ref, own_t_ref, prv_t_ref, nxt_t_ref,
):
    halo = (prv_ref.shape[0] - 16) // 3
    own_n = rest_ref.shape[1]
    pieces = [jnp.concatenate([rest_ref[...], mass_ref[...]], axis=0)]
    for ref in (prv_ref, nxt_ref):
        tail = ref[3 * halo :, :halo].astype(F32)
        pieces.append(
            jnp.concatenate([tail[0:3] + tail[3:6] + tail[6:9], jnp.zeros((1, halo), F32)], axis=0)
        )
    cols = column_block(jnp.concatenate(pieces, axis=1))
    edge_ref[...] = exact_dot(d_ref[...], cols)
    stretch = exact_dot(b_ref[...], cols) - column_block(bend_ref[...])
    force = exact_dot(bt_ref[...], stretch) * (2.0 * BENDING / frames)
    lane = lax.broadcasted_iota(jnp.int32, cols.shape, 1)
    weight = jnp.sum(jnp.where(lane == 3, cols, 0.0), axis=1, keepdims=True) * (GRAVITY / frames)
    vert_ref[...] = force + jnp.where(lane == 2, weight, 0.0)
    sqc_ref[...] = column_block(sq_ref[...])
    for c in range(3):
        own_t_ref[:, c * own_n : (c + 1) * own_n] = own_ref[c].T
    prv_t_ref[...] = prv_ref[: 3 * halo, :].T
    nxt_t_ref[...] = nxt_ref[: 3 * halo, :].T


def elastic_kernel(
    frames, step,
    core_ref, mine_ref, sib_ref, own_ref, prv_ref, nxt_ref, d_ref, dt_ref, lap_ref, edge_ref,
    vert_ref, sq_ref,
    lat_ref, f_own_ref, f_prv_ref, f_nxt_ref,
):
    own_n = own_ref.shape[1]
    t = sq_ref.shape[0]
    halo = f_prv_ref.shape[0] // 3
    interleave(core_ref[0], mine_ref, sib_ref, lat_ref)
    scale = 4.0 * MEMBRANE / frames
    for at in range(0, lat_ref.shape[1], step):
        here = slice(at, at + step)
        lat = lat_ref[:, here]
        x_prv = dot(prv_ref[: 3 * halo, :], lat).astype(BF)
        x_nxt = dot(nxt_ref[: 3 * halo, :], lat).astype(BF)
        points, edges = [], []
        for c in range(3):
            x = jnp.concatenate(
                [
                    dot(own_ref[c], lat).astype(BF),
                    x_prv[c * halo : (c + 1) * halo],
                    x_nxt[c * halo : (c + 1) * halo],
                ],
                axis=0,
            )
            points.append(x)
            edges.append(dot(d_ref[...], x) + edge_ref[:, c : c + 1])
        e1 = [e[:t] for e in edges]
        e2 = [e[t:] for e in edges]
        e3 = [u + v for u, v in zip(e1, e2)]
        s1, s2, s3 = (
            scale * (e[0] * e[0] + e[1] * e[1] + e[2] * e[2] - sq_ref[:, i : i + 1])
            for i, e in enumerate((e1, e2, e3))
        )
        for c in range(3):
            third = s3 * e3[c]
            g = jnp.concatenate(
                [(s1 * e1[c] + third).astype(BF), (s2 * e2[c] + third).astype(BF)], axis=0
            )
            f = dot(dt_ref[...], g) + dot(lap_ref[...], points[c]) * (2.0 * BENDING / frames)
            f = f + vert_ref[:, c : c + 1]
            f_own_ref[c * own_n : (c + 1) * own_n, here] = f[:own_n]
            f_prv_ref[c * halo : (c + 1) * halo, here] = f[own_n : own_n + halo].astype(BF)
            f_nxt_ref[c * halo : (c + 1) * halo, here] = f[own_n + halo :].astype(BF)


def latent_kernel(own_t_ref, prv_t_ref, nxt_t_ref, f_own_ref, f_prv_ref, f_nxt_ref, lg_ref):
    lg = dot(own_t_ref[...], f_own_ref[...].astype(BF))
    lg = lg + dot(prv_t_ref[...], f_prv_ref[...]) + dot(nxt_t_ref[...], f_nxt_ref[...])
    lg_ref[...] = lg.astype(BF)


def adjoint_kernel(
    half_ref, send_ref, f_own_ref, back_prv_ref, back_nxt_ref, mine_ref, other_ref
):
    halo = send_ref.shape[1]
    own = f_own_ref.shape[0] // 3
    half = own // 2
    first = half_ref[0] == 0
    to_prev = one_hot(own, send_ref[0:1, :]).astype(BF)
    to_next = one_hot(own, send_ref[1:2, :]).astype(BF)
    for c in range(3):
        rows = slice(c * halo, (c + 1) * halo)
        total = f_own_ref[c * own : (c + 1) * own, :]
        total = total + dot(to_prev, back_prv_ref[rows, :]) + dot(to_next, back_nxt_ref[rows, :])
        low, high = total[:half], total[half:]
        mine_ref[c * half : (c + 1) * half, :] = jnp.where(first, low, high).astype(BF)
        other_ref[c * half : (c + 1) * half, :] = jnp.where(first, high, low).astype(BF)


def own_part_kernel(mine_ref, lat_ref, out_ref):
    out_ref[...] = dot(mine_ref[...], lat_ref[...], NT).astype(BF)


def basis_grad_kernel(core_ref, part_ref, far_ref, core_lat_ref, sib_lat_ref, out_ref, lat_ref):
    interleave(core_ref[0], core_lat_ref, sib_lat_ref, lat_ref)
    far = dot(far_ref[...], lat_ref[...], NT).astype(BF).astype(F32)
    out_ref[...] = part_ref[...].astype(F32) + far


SMEM = pl.BlockSpec(memory_space=pltpu.SMEM)
VMEM = pl.BlockSpec(memory_space=pltpu.VMEM)


def call(kernel, outs, *args, scalars=0, scratch=()):
    return pl.pallas_call(
        kernel,
        in_specs=[SMEM] * scalars + [VMEM] * (len(args) - scalars),
        out_specs=[VMEM] * len(outs),
        out_shape=[jax.ShapeDtypeStruct(s, d) for s, d in outs],
        scratch_shapes=list(scratch),
        compiler_params=PARAMS,
    )(*args)


def local(basis, latents, rest_pos, triangles, hinges, rest_sq, bend_rest, masses, send_rows):
    own = basis.shape[1]
    width = basis.shape[2]
    frames = latents.shape[0]
    each = latents.shape[1]
    halo = send_rows.shape[1]
    tris = triangles.shape[1]
    hings = hinges.shape[1]
    ext = own + 2 * halo
    half = own // 2
    patches = lax.axis_size("patch")
    total_frames = frames * lax.axis_size("frame")
    chips = patches // 2
    onward = [(i, (i + 1) % patches) for i in range(patches)]
    backward = [((i + 1) % patches, i) for i in range(patches)]
    sibling = [(i, i ^ 1) for i in range(patches)]
    partner = [(0, 1), (1, 0)]
    same_core = [[2 * i + c for i in range(chips)] for c in range(2)]
    core = (lax.axis_index("patch") % 2).astype(jnp.int32).reshape(1)
    half_index = lax.axis_index("frame").astype(jnp.int32).reshape(1)

    lat_core = lax.all_to_all(
        jnp.broadcast_to(latents.T[None], (chips, each, frames)),
        "patch", 0, 0, tiled=True, axis_index_groups=same_core,
    )
    sent = ((3 * halo + 16, width), BF)
    rows_prev, rows_next = call(pick_kernel, [sent, sent], send_rows, basis, rest_pos)
    halo_prv = lax.ppermute(rows_next, "patch", onward)
    halo_nxt = lax.ppermute(rows_prev, "patch", backward)
    d, dt, b, bt, lap = call(
        incidence_kernel,
        [
            ((2 * tris, ext), BF),
            ((ext, 2 * tris), BF),
            ((hings, ext), BF),
            ((ext, hings), BF),
            ((ext, ext), BF),
        ],
        triangles,
        hinges,
    )
    edge, vert, sq, own_t, prv_t, nxt_t = call(
        functools.partial(constants_kernel, total_frames),
        [
            ((2 * tris, 128), F32),
            ((ext, 128), F32),
            ((tris, 128), F32),
            ((width, 3 * own), BF),
            ((width, 3 * halo), BF),
            ((width, 3 * halo), BF),
        ],
        rest_pos, masses[None], halo_prv, halo_nxt, bend_rest, rest_sq, d, b, bt, basis,
    )
    lat_sib = lax.ppermute(lat_core, "patch", sibling)
    lat_all, f_own, f_prv, f_nxt = call(
        functools.partial(elastic_kernel, total_frames, min(frames, 256)),
        [
            ((width, frames), BF),
            ((3 * own, frames), F32),
            ((3 * halo, frames), BF),
            ((3 * halo, frames), BF),
        ],
        core, lat_core, lat_sib, basis, halo_prv, halo_nxt, d, dt, lap, edge, vert, sq,
        scalars=1,
    )

    back_nxt = lax.ppermute(f_prv, "patch", backward)
    back_prv = lax.ppermute(f_nxt, "patch", onward)

    [lg] = call(
        latent_kernel, [((width, frames), BF)], own_t, prv_t, nxt_t, f_own, f_prv, f_nxt
    )
    shares = lax.all_to_all(lg.reshape(patches, each, frames), "patch", 0, 0, tiled=True)
    latent_grad = jnp.sum(shares.astype(F32), axis=0).T

    far_core = lax.ppermute(lat_core, "frame", partner)
    far_sib = lax.ppermute(far_core, "patch", sibling)

    piece = ((3 * half, frames), BF)
    mine, other = call(
        adjoint_kernel, [piece, piece], half_index, send_rows, f_own, back_prv, back_nxt,
        scalars=1,
    )
    received = lax.ppermute(other, "frame", partner)
    [part] = call(own_part_kernel, [((3 * half, width), BF)], mine, lat_all)
    [basis_grad] = call(
        basis_grad_kernel, [((3 * half, width), F32)], core, part, received, far_core, far_sib,
        scalars=1, scratch=[pltpu.VMEM((width, frames), BF)],
    )
    return basis_grad.reshape(3, half, width), latent_grad


def solution(mesh):
    return jax.shard_map(
        local,
        mesh=mesh,
        in_specs=(
            P(None, "patch", None),
            P("frame", "patch"),
            P(None, "patch"),
            P(None, "patch"),
            P(None, "patch"),
            P(None, "patch"),
            P(None, "patch"),
            P("patch"),
            P(None, "patch"),
        ),
        out_specs=(P(None, ("patch", "frame"), None), P("frame", "patch")),
        check_vma=False,
    )
```

```python
import functools
import math

import jax
import jax.numpy as jnp
from jax import lax
from jax.experimental import pallas as pl
from jax.experimental.pallas import tpu as pltpu
from jax.sharding import PartitionSpec as P

MEMBRANE = 5.0
BENDING = 5.0
GRAVITY = 40.0
BF = jnp.bfloat16
F32 = jnp.float32
NN = (((1,), (0,)), ((), ()))
TN = (((0,), (0,)), ((), ()))
NT = (((1,), (1,)), ((), ()))


def dot(a, b, dims=NN):
    return lax.dot_general(a, b, dims, preferred_element_type=F32)


def exact_dot(a, b):
    total = None
    for _ in range(3):
        part = b.astype(BF)
        b = b - part.astype(F32)
        term = dot(a, part)
        total = term if total is None else total + term
    return total


def one_hot(rows, ids):
    return (lax.broadcasted_iota(jnp.int32, (rows, ids.shape[1]), 0) == ids).astype(F32)


def column_block(rows):
    n, width = rows.shape
    return jnp.concatenate([rows, jnp.zeros((128 - n, width), F32)], axis=0).T


def interleave(core, mine_ref, other_ref, out_ref):
    chips, each, _ = mine_ref.shape
    for i in range(chips):
        out_ref[pl.ds(pl.multiple_of((2 * i + core) * each, each), each), :] = mine_ref[i]
        out_ref[pl.ds(pl.multiple_of((2 * i + 1 - core) * each, each), each), :] = other_ref[i]


def send(ref):
    if isinstance(ref, Stored):
        ref.send()


def first_kernel(shard_ref, send_ref, basis_ref, rest_ref, copies_ref, prev_ref, next_ref):
    for i in range(copies_ref.shape[0]):
        copies_ref[i] = shard_ref[...]
    send(copies_ref)
    own, halo = basis_ref.shape[1], send_ref.shape[1]
    rest = rest_ref[...]
    parts = []
    for _ in range(3):
        part = rest.astype(BF)
        rest = rest - part.astype(F32)
        parts.append(part.astype(F32))
    parts.append(jnp.zeros((7, own), F32))
    parts = jnp.concatenate(parts, axis=0).astype(BF)
    for row, out in ((0, prev_ref), (1, next_ref)):
        sel = one_hot(own, send_ref[row : row + 1, :]).astype(BF)
        for c in range(3):
            out[c * halo : (c + 1) * halo, :] = dot(sel, basis_ref[c], TN).astype(BF)
        out[3 * halo :, :] = jnp.zeros((out.shape[0] - 3 * halo, out.shape[1]), BF)
        out[3 * halo :, :halo] = dot(parts, sel).astype(BF)
        send(out)


def own_kernel(
    tri_ref, hin_ref, sq_ref, own_ref, d_ref, dt_ref, b_ref, bt_ref, lap_ref, sqc_ref, own_t_ref
):
    ext = dt_ref.shape[0]
    own_n = own_ref.shape[1]
    sqc_ref[...] = column_block(sq_ref[...])
    for c in range(3):
        own_t_ref[:, c * own_n : (c + 1) * own_n] = own_ref[c].T
    t = tri_ref.shape[1]
    a, b, c = (one_hot(ext, tri_ref[i : i + 1, :]) for i in range(3))
    for at, part in ((0, b - a), (t, c - b)):
        dt_ref[:, at : at + t] = part.astype(BF)
        d_ref[at : at + t, :] = part.T.astype(BF)
    a, b, c, d = (one_hot(ext, hin_ref[i : i + 1, :]) for i in range(4))
    part = c + d - a - b
    bt_ref[...] = part.astype(BF)
    b_ref[...] = part.T.astype(BF)
    lap_ref[...] = dot(bt_ref[...], b_ref[...]).astype(BF)


def halo_kernel(
    frames,
    rest_ref, mass_ref, prv_ref, nxt_ref, bend_ref, d_ref, b_ref, bt_ref,
    edge_ref, vert_ref, halo_t_ref,
):
    halo = (prv_ref.shape[0] - 16) // 3
    pieces = [jnp.concatenate([rest_ref[...], mass_ref[...]], axis=0)]
    for ref in (prv_ref, nxt_ref):
        tail = ref[3 * halo :, :halo].astype(F32)
        pieces.append(
            jnp.concatenate([tail[0:3] + tail[3:6] + tail[6:9], jnp.zeros((1, halo), F32)], axis=0)
        )
    cols = column_block(jnp.concatenate(pieces, axis=1))
    edge_ref[...] = exact_dot(d_ref[...], cols)
    stretch = exact_dot(b_ref[...], cols) - column_block(bend_ref[...])
    force = exact_dot(bt_ref[...], stretch) * (2.0 * BENDING / frames)
    lane = lax.broadcasted_iota(jnp.int32, cols.shape, 1)
    weight = jnp.sum(jnp.where(lane == 3, cols, 0.0), axis=1, keepdims=True) * (GRAVITY / frames)
    vert_ref[...] = force + jnp.where(lane == 2, weight, 0.0)
    halo_t_ref[:, : 3 * halo] = prv_ref[: 3 * halo, :].T
    halo_t_ref[:, 3 * halo :] = nxt_ref[: 3 * halo, :].T


def elastic_kernel(
    frames, step,
    core_ref, mine_ref, sib_ref, own_ref, prv_ref, nxt_ref, d_ref, dt_ref, lap_ref, edge_ref,
    vert_ref, sq_ref, own_t_ref, halo_t_ref,
    lat_ref, f_own_ref, f_prv_ref, f_nxt_ref, lg_ref, f_all_ref,
):
    own_n = own_ref.shape[1]
    t = sq_ref.shape[0]
    halo = f_prv_ref.shape[0] // 3
    interleave(core_ref[0], mine_ref, sib_ref, lat_ref)
    scale = 4.0 * MEMBRANE / frames
    for at in range(0, lat_ref.shape[1], step):
        here = slice(at, at + step)
        lat = lat_ref[:, here]
        x_prv = dot(prv_ref[: 3 * halo, :], lat).astype(BF)
        x_nxt = dot(nxt_ref[: 3 * halo, :], lat).astype(BF)
        points, edges = [], []
        for c in range(3):
            x = jnp.concatenate(
                [
                    dot(own_ref[c], lat).astype(BF),
                    x_prv[c * halo : (c + 1) * halo],
                    x_nxt[c * halo : (c + 1) * halo],
                ],
                axis=0,
            )
            points.append(x)
            edges.append(dot(d_ref[...], x) + edge_ref[:, c : c + 1])
        e1 = [e[:t] for e in edges]
        e2 = [e[t:] for e in edges]
        e3 = [u + v for u, v in zip(e1, e2)]
        s1, s2, s3 = (
            scale * (e[0] * e[0] + e[1] * e[1] + e[2] * e[2] - sq_ref[:, i : i + 1])
            for i, e in enumerate((e1, e2, e3))
        )
        for c in range(3):
            third = s3 * e3[c]
            g = jnp.concatenate(
                [(s1 * e1[c] + third).astype(BF), (s2 * e2[c] + third).astype(BF)], axis=0
            )
            f = dot(dt_ref[...], g) + dot(lap_ref[...], points[c]) * (2.0 * BENDING / frames)
            f = f + vert_ref[:, c : c + 1]
            f_own_ref[c * own_n : (c + 1) * own_n, here] = f[:own_n]
            short = f.astype(BF)
            f_prv_ref[c * halo : (c + 1) * halo, here] = short[own_n : own_n + halo]
            f_nxt_ref[c * halo : (c + 1) * halo, here] = short[own_n + halo :]
            for at_row, size, first in (
                (c * own_n, own_n, 0),
                (3 * own_n + c * halo, halo, own_n),
                (3 * (own_n + halo) + c * halo, halo, own_n + halo),
            ):
                f_all_ref[at_row : at_row + size, here] = short[first : first + size]
    for at in range(0, lg_ref.shape[0], 256):
        rows = slice(at, at + 256)
        both = jnp.concatenate([own_t_ref[rows, :], halo_t_ref[rows, :]], axis=1)
        lg_ref[rows, :] = dot(both, f_all_ref[...]).astype(BF)


def share_kernel(shares_ref, out_ref):
    total = shares_ref[0].astype(F32)
    for i in range(1, shares_ref.shape[0]):
        total = total + shares_ref[i].astype(F32)
    out_ref[...] = total


def adjoint_kernel(
    half_ref, send_ref, f_own_ref, back_prv_ref, back_nxt_ref, mine_ref, other_ref
):
    halo = send_ref.shape[1]
    own = f_own_ref.shape[0] // 3
    half = own // 2
    first = half_ref[0] == 0
    to_prev = one_hot(own, send_ref[0:1, :]).astype(BF)
    to_next = one_hot(own, send_ref[1:2, :]).astype(BF)
    for c in range(3):
        rows = slice(c * halo, (c + 1) * halo)
        total = f_own_ref[c * own : (c + 1) * own, :]
        total = total + dot(to_prev, back_prv_ref[rows, :]) + dot(to_next, back_nxt_ref[rows, :])
        low, high = total[:half], total[half:]
        mine_ref[c * half : (c + 1) * half, :] = jnp.where(first, low, high).astype(BF)
        other_ref[c * half : (c + 1) * half, :] = jnp.where(first, high, low).astype(BF)


def own_part_kernel(mine_ref, lat_ref, out_ref):
    out_ref[...] = dot(mine_ref[...], lat_ref[...], NT).astype(BF)


def basis_grad_kernel(core_ref, part_ref, far_ref, core_lat_ref, sib_lat_ref, out_ref, lat_ref):
    interleave(core_ref[0], core_lat_ref, sib_lat_ref, lat_ref)
    far = dot(far_ref[...], lat_ref[...], NT).astype(BF).astype(F32)
    out_ref[...] = part_ref[...].astype(F32) + far


class Loaded:
    def __init__(self, source, ref, sem):
        self.ref, self.copy = ref, pltpu.make_async_copy(source, ref, sem)
        self.shape, self.waiting = ref.shape, True
        self.copy.start()

    def wait(self):
        if self.waiting:
            self.copy.wait()
            self.waiting = False

    def __getitem__(self, index):
        self.wait()
        return self.ref[index]


class Stored:
    def __init__(self, ref, target, sem):
        self.ref, self.copy = ref, pltpu.make_async_copy(ref, target, sem)
        self.shape, self.open = ref.shape, True

    def __setitem__(self, index, value):
        self.ref[index] = value

    def __getitem__(self, index):
        return self.ref[index]

    def send(self):
        if self.open:
            self.copy.start()
            self.open = False


SMEM = pl.BlockSpec(memory_space=pltpu.SMEM)
ANY = pl.BlockSpec(memory_space=pl.ANY)
VMEM = pl.BlockSpec(memory_space=pltpu.VMEM)


def call(kernel, outs, *args, scalars=0, direct=True, near=(), scratch=(), macs=0, room=0):
    moved = sum(a.size * a.dtype.itemsize for a in args)
    moved += sum(math.prod(s) * jnp.dtype(d).itemsize for s, d in outs)
    ins, n_in, n_out = args[scalars:], len(args) - scalars, len(outs)
    params = pltpu.CompilerParams(vmem_limit_bytes=(room or 24) << 20)
    if direct:
        return pl.pallas_call(
            kernel,
            cost_estimate=pl.CostEstimate(flops=2 * macs, bytes_accessed=moved, transcendentals=0),
            in_specs=[SMEM] * scalars + [VMEM] * n_in,
            out_specs=[VMEM] * n_out,
            out_shape=[jax.ShapeDtypeStruct(s, d) for s, d in outs],
            scratch_shapes=list(scratch),
            compiler_params=params,
        )(*args)
    far = [i for i in range(n_in) if i + scalars not in near]
    n_far = len(far)

    def body(*refs):
        numbers, refs = refs[:scalars], refs[scalars:]
        sources, targets, refs = refs[:n_in], refs[n_in : n_in + n_out], refs[n_in + n_out :]
        held, made, refs = refs[:n_far], refs[n_far : n_far + n_out], refs[n_far + n_out :]
        in_sem, out_sem, *rest = refs
        loads = list(sources)
        for i, at in enumerate(far):
            loads[at] = Loaded(sources[at], held[i], in_sem.at[i])
        stores = [Stored(v, x, out_sem.at[i]) for i, (x, v) in enumerate(zip(targets, made))]
        kernel(*numbers, *loads, *stores, *rest)
        for at in far:
            loads[at].wait()
        for store in stores:
            store.send()
        for store in stores:
            store.copy.wait()

    return pl.pallas_call(
        body,
        cost_estimate=pl.CostEstimate(flops=2 * macs, bytes_accessed=moved, transcendentals=0),
        in_specs=[SMEM] * scalars + [ANY if i in far else VMEM for i in range(n_in)],
        out_specs=[ANY] * n_out,
        out_shape=[jax.ShapeDtypeStruct(s, d) for s, d in outs],
        scratch_shapes=[pltpu.VMEM(ins[i].shape, ins[i].dtype) for i in far]
        + [pltpu.VMEM(s, d) for s, d in outs]
        + [pltpu.SemaphoreType.DMA((max(n_far, 1),)), pltpu.SemaphoreType.DMA((n_out,))]
        + list(scratch),
        compiler_params=params,
    )(*args)


def local(basis, latents, rest_pos, triangles, hinges, rest_sq, bend_rest, masses, send_rows):
    own = basis.shape[1]
    width = basis.shape[2]
    frames = latents.shape[0]
    each = latents.shape[1]
    halo = send_rows.shape[1]
    tris = triangles.shape[1]
    hings = hinges.shape[1]
    ext = own + 2 * halo
    half = own // 2
    patches = lax.axis_size("patch")
    total_frames = frames * lax.axis_size("frame")
    chips = patches // 2
    onward = [(i, (i + 1) % patches) for i in range(patches)]
    backward = [((i + 1) % patches, i) for i in range(patches)]
    sibling = [(i, i ^ 1) for i in range(patches)]
    partner = [(0, 1), (1, 0)]
    same_core = [[2 * i + c for i in range(chips)] for c in range(2)]
    core = (lax.axis_index("patch") % 2).astype(jnp.int32).reshape(1)
    half_index = lax.axis_index("frame").astype(jnp.int32).reshape(1)

    sent = ((3 * halo + 16, width), BF)
    copies, rows_prev, rows_next = call(
        first_kernel, [((chips, each, frames), BF), sent, sent],
        latents.T, send_rows, basis, rest_pos, direct=False, room=60,
    )
    lat_core = lax.all_to_all(
        copies, "patch", 0, 0, tiled=True, axis_index_groups=same_core
    )
    halo_prv = lax.ppermute(rows_next, "patch", onward)
    halo_nxt = lax.ppermute(rows_prev, "patch", backward)
    d, dt, b, bt, lap, sq, own_t = call(
        own_kernel,
        [
            ((2 * tris, ext), BF),
            ((ext, 2 * tris), BF),
            ((hings, ext), BF),
            ((ext, hings), BF),
            ((ext, ext), BF),
            ((tris, 128), F32),
            ((width, 3 * own), BF),
        ],
        triangles, hinges, rest_sq, basis,
        macs=1 << 30,
    )
    edge, vert, halo_t = call(
        functools.partial(halo_kernel, total_frames),
        [((2 * tris, 128), F32), ((ext, 128), F32), ((width, 6 * halo), BF)],
        rest_pos, masses[None], halo_prv, halo_nxt, bend_rest, d, b, bt,
        macs=1 << 30,
    )
    lat_sib = lax.ppermute(lat_core, "patch", sibling)
    lat_all, f_own, f_prv, f_nxt, lg = call(
        functools.partial(elastic_kernel, total_frames, min(frames, 256)),
        [
            ((width, frames), BF),
            ((3 * own, frames), F32),
            ((3 * halo, frames), BF),
            ((3 * halo, frames), BF),
            ((width, frames), BF),
        ],
        core, lat_core, lat_sib, basis, halo_prv, halo_nxt, d, dt, lap, edge, vert, sq,
        own_t, halo_t,
        scalars=1, scratch=[pltpu.VMEM((3 * ext, frames), BF)], macs=5 << 30, room=32,
    )

    back_nxt = lax.ppermute(f_prv, "patch", backward)
    back_prv = lax.ppermute(f_nxt, "patch", onward)

    shares = lax.all_to_all(lg.reshape(patches, each, frames), "patch", 0, 0, tiled=True)
    [latent_grad] = call(share_kernel, [((each, frames), F32)], shares)

    far_core = lax.ppermute(lat_core, "frame", partner)
    far_sib = lax.ppermute(far_core, "patch", sibling)

    piece = ((3 * half, frames), BF)
    mine, other = call(
        adjoint_kernel, [piece, piece], half_index, send_rows, f_own, back_prv, back_nxt,
        scalars=1, macs=10 << 30,
    )
    received = lax.ppermute(other, "frame", partner)
    [part] = call(own_part_kernel, [((3 * half, width), BF)], mine, lat_all, macs=3 * half * width * frames)
    [basis_grad] = call(
        basis_grad_kernel, [((3 * half, width), F32)], core, part, received, far_core, far_sib,
        scalars=1, scratch=[pltpu.VMEM((width, frames), BF)],
    )
    return basis_grad.reshape(3, half, width), latent_grad.T


def solution(mesh):
    return jax.shard_map(
        local,
        mesh=mesh,
        in_specs=(
            P(None, "patch", None),
            P("frame", "patch"),
            P(None, "patch"),
            P(None, "patch"),
            P(None, "patch"),
            P(None, "patch"),
            P(None, "patch"),
            P("patch"),
            P(None, "patch"),
        ),
        out_specs=(P(None, ("patch", "frame"), None), P("frame", "patch")),
        check_vma=False,
    )
```

```python
import functools
import math

import jax
import jax.numpy as jnp
from jax import lax
from jax.experimental import pallas as pl
from jax.experimental.pallas import tpu as pltpu
from jax.sharding import PartitionSpec as P

MEMBRANE = 5.0
BENDING = 5.0
GRAVITY = 40.0
BF = jnp.bfloat16
F32 = jnp.float32
NN = (((1,), (0,)), ((), ()))
TN = (((0,), (0,)), ((), ()))
NT = (((1,), (1,)), ((), ()))


def dot(a, b, dims=NN):
    return lax.dot_general(a, b, dims, preferred_element_type=F32)


def exact_dot(a, b):
    total = None
    for _ in range(3):
        part = b.astype(BF)
        b = b - part.astype(F32)
        term = dot(a, part)
        total = term if total is None else total + term
    return total


def one_hot(rows, ids):
    return (lax.broadcasted_iota(jnp.int32, (rows, ids.shape[1]), 0) == ids).astype(F32)


def column_block(rows):
    n, width = rows.shape
    return jnp.concatenate([rows, jnp.zeros((128 - n, width), F32)], axis=0).T


def interleave(core, mine_ref, other_ref, out_ref):
    chips, each, _ = mine_ref.shape
    for i in range(chips):
        out_ref[pl.ds(pl.multiple_of((2 * i + core) * each, each), each), :] = mine_ref[i]
        out_ref[pl.ds(pl.multiple_of((2 * i + 1 - core) * each, each), each), :] = other_ref[i]


def copies_kernel(shard_ref, copies_ref):
    for i in range(copies_ref.shape[0]):
        copies_ref[i] = shard_ref[...]


def rows_kernel(send_ref, basis_ref, rest_ref, prev_ref, next_ref):
    own, halo = basis_ref.shape[1], send_ref.shape[1]
    rest = rest_ref[...]
    parts = []
    for _ in range(3):
        part = rest.astype(BF)
        rest = rest - part.astype(F32)
        parts.append(part.astype(F32))
    parts.append(jnp.zeros((7, own), F32))
    parts = jnp.concatenate(parts, axis=0).astype(BF)
    for row, out in ((0, prev_ref), (1, next_ref)):
        sel = one_hot(own, send_ref[row : row + 1, :]).astype(BF)
        for c in range(3):
            out[c * halo : (c + 1) * halo, :] = dot(sel, basis_ref[c], TN).astype(BF)
        out[3 * halo :, :] = jnp.zeros((out.shape[0] - 3 * halo, out.shape[1]), BF)
        out[3 * halo :, :halo] = dot(parts, sel).astype(BF)


def own_kernel(
    tri_ref, hin_ref, sq_ref, own_ref, d_ref, dt_ref, b_ref, bt_ref, lap_ref, sqc_ref, own_t_ref
):
    ext = dt_ref.shape[0]
    own_n = own_ref.shape[1]
    sqc_ref[...] = column_block(sq_ref[...])
    for c in range(3):
        own_t_ref[:, c * own_n : (c + 1) * own_n] = own_ref[c].T
    t = tri_ref.shape[1]
    a, b, c = (one_hot(ext, tri_ref[i : i + 1, :]) for i in range(3))
    for at, part in ((0, b - a), (t, c - b)):
        dt_ref[:, at : at + t] = part.astype(BF)
        d_ref[at : at + t, :] = part.T.astype(BF)
    a, b, c, d = (one_hot(ext, hin_ref[i : i + 1, :]) for i in range(4))
    part = c + d - a - b
    bt_ref[...] = part.astype(BF)
    b_ref[...] = part.T.astype(BF)
    lap_ref[...] = dot(bt_ref[...], b_ref[...]).astype(BF)


def halo_kernel(
    frames,
    rest_ref, mass_ref, prv_ref, nxt_ref, bend_ref, d_ref, b_ref, bt_ref,
    edge_ref, vert_ref, halo_t_ref,
):
    halo = (prv_ref.shape[0] - 16) // 3
    pieces = [jnp.concatenate([rest_ref[...], mass_ref[...]], axis=0)]
    for ref in (prv_ref, nxt_ref):
        tail = ref[3 * halo :, :halo].astype(F32)
        pieces.append(
            jnp.concatenate([tail[0:3] + tail[3:6] + tail[6:9], jnp.zeros((1, halo), F32)], axis=0)
        )
    cols = column_block(jnp.concatenate(pieces, axis=1))
    edge_ref[...] = exact_dot(d_ref[...], cols)
    stretch = exact_dot(b_ref[...], cols) - column_block(bend_ref[...])
    force = exact_dot(bt_ref[...], stretch) * (2.0 * BENDING / frames)
    lane = lax.broadcasted_iota(jnp.int32, cols.shape, 1)
    weight = jnp.sum(jnp.where(lane == 3, cols, 0.0), axis=1, keepdims=True) * (GRAVITY / frames)
    vert_ref[...] = force + jnp.where(lane == 2, weight, 0.0)
    halo_t_ref[:, : 3 * halo] = prv_ref[: 3 * halo, :].T
    halo_t_ref[:, 3 * halo :] = nxt_ref[: 3 * halo, :].T


def elastic_kernel(
    frames, step,
    core_ref, mine_ref, sib_ref, own_ref, prv_ref, nxt_ref, d_ref, dt_ref, lap_ref, edge_ref,
    vert_ref, sq_ref, own_t_ref, halo_t_ref,
    lat_ref, f_own_ref, f_prv_ref, f_nxt_ref, keep_ref, give_ref, f_all_ref,
):
    own_n = own_ref.shape[1]
    t = sq_ref.shape[0]
    halo = f_prv_ref.shape[0] // 3
    interleave(core_ref[0], mine_ref, sib_ref, lat_ref)
    scale = 4.0 * MEMBRANE / frames
    for at in range(0, lat_ref.shape[1], step):
        here = slice(at, at + step)
        lat = lat_ref[:, here]
        x_prv = dot(prv_ref[: 3 * halo, :], lat).astype(BF)
        x_nxt = dot(nxt_ref[: 3 * halo, :], lat).astype(BF)
        points, edges = [], []
        for c in range(3):
            x = jnp.concatenate(
                [
                    dot(own_ref[c], lat).astype(BF),
                    x_prv[c * halo : (c + 1) * halo],
                    x_nxt[c * halo : (c + 1) * halo],
                ],
                axis=0,
            )
            points.append(x)
            edges.append(dot(d_ref[...], x) + edge_ref[:, c : c + 1])
        e1 = [e[:t] for e in edges]
        e2 = [e[t:] for e in edges]
        e3 = [u + v for u, v in zip(e1, e2)]
        s1, s2, s3 = (
            scale * (e[0] * e[0] + e[1] * e[1] + e[2] * e[2] - sq_ref[:, i : i + 1])
            for i, e in enumerate((e1, e2, e3))
        )
        for c in range(3):
            third = s3 * e3[c]
            g = jnp.concatenate(
                [(s1 * e1[c] + third).astype(BF), (s2 * e2[c] + third).astype(BF)], axis=0
            )
            f = dot(dt_ref[...], g) + dot(lap_ref[...], points[c]) * (2.0 * BENDING / frames)
            f = f + vert_ref[:, c : c + 1]
            f_own_ref[c * own_n : (c + 1) * own_n, here] = f[:own_n]
            short = f.astype(BF)
            f_prv_ref[c * halo : (c + 1) * halo, here] = short[own_n : own_n + halo]
            f_nxt_ref[c * halo : (c + 1) * halo, here] = short[own_n + halo :]
            for at_row, size, first in (
                (c * own_n, own_n, 0),
                (3 * own_n + c * halo, halo, own_n),
                (3 * (own_n + halo) + c * halo, halo, own_n + halo),
            ):
                f_all_ref[at_row : at_row + size, here] = short[first : first + size]
    each = mine_ref.shape[1]
    first = core_ref[0] == 0
    for at in range(0, lat_ref.shape[0], 256):
        rows = slice(at, at + 256)
        both = jnp.concatenate([own_t_ref[rows, :], halo_t_ref[rows, :]], axis=1)
        block = dot(both, f_all_ref[...])
        for i in range(0, 256, 2 * each):
            low, high = block[i : i + each], block[i + each : i + 2 * each]
            chip = (at + i) // (2 * each)
            keep_ref[chip] = jnp.where(first, low, high).astype(BF)
            give_ref[chip] = jnp.where(first, high, low).astype(BF)


def pair_kernel(a_ref, b_ref, out_ref):
    out_ref[...] = (a_ref[...].astype(F32) + b_ref[...].astype(F32)).astype(BF)


def share_kernel(shares_ref, out_ref):
    total = shares_ref[0].astype(F32)
    for i in range(1, shares_ref.shape[0]):
        total = total + shares_ref[i].astype(F32)
    out_ref[...] = total


def adjoint_kernel(
    half_ref, send_ref, f_own_ref, back_prv_ref, back_nxt_ref, mine_ref, other_ref
):
    halo = send_ref.shape[1]
    own = f_own_ref.shape[0] // 3
    half = own // 2
    first = half_ref[0] == 0
    to_prev = one_hot(own, send_ref[0:1, :]).astype(BF)
    to_next = one_hot(own, send_ref[1:2, :]).astype(BF)
    for c in range(3):
        rows = slice(c * halo, (c + 1) * halo)
        total = f_own_ref[c * own : (c + 1) * own, :]
        total = total + dot(to_prev, back_prv_ref[rows, :]) + dot(to_next, back_nxt_ref[rows, :])
        low, high = total[:half], total[half:]
        mine_ref[c * half : (c + 1) * half, :] = jnp.where(first, low, high).astype(BF)
        other_ref[c * half : (c + 1) * half, :] = jnp.where(first, high, low).astype(BF)


def own_part_far_kernel(core_ref, mine_ref, lat_ref, core_lat_ref, sib_lat_ref, out_ref, far_lat_ref):
    interleave(core_ref[0], core_lat_ref, sib_lat_ref, far_lat_ref)
    out_ref[...] = dot(mine_ref[...], lat_ref[...], NT).astype(BF)


def last_kernel(part_ref, far_ref, lat_ref, done_ref, out_ref, sum_ref, sem):
    third = out_ref.shape[0] // 3
    copies = []
    for c in range(3):
        rows = slice(c * third, (c + 1) * third)
        far = dot(far_ref[rows, :], lat_ref[...], NT).astype(BF).astype(F32)
        sum_ref[rows, :] = part_ref[rows, :].astype(F32) + far
        copies.append(pltpu.make_async_copy(sum_ref.at[rows], out_ref.at[rows], sem.at[c]))
        copies[-1].start()
    for copy in copies:
        copy.wait()


SMEM = pl.BlockSpec(memory_space=pltpu.SMEM)
ANY = pl.BlockSpec(memory_space=pl.ANY)
VMEM = pl.BlockSpec(memory_space=pltpu.VMEM)


def call(kernel, outs, *args, scalars=0, macs=0, room=24, scratch=()):
    moved = sum(a.size * a.dtype.itemsize for a in args)
    moved += sum(math.prod(s) * jnp.dtype(d).itemsize for s, d in outs)
    return pl.pallas_call(
        kernel,
        cost_estimate=pl.CostEstimate(flops=2 * macs, bytes_accessed=moved, transcendentals=0),
        in_specs=[SMEM] * scalars + [VMEM] * (len(args) - scalars),
        out_specs=[VMEM] * len(outs),
        out_shape=[jax.ShapeDtypeStruct(s, d) for s, d in outs],
        scratch_shapes=list(scratch),
        compiler_params=pltpu.CompilerParams(vmem_limit_bytes=room << 20),
    )(*args)


def local(basis, latents, rest_pos, triangles, hinges, rest_sq, bend_rest, masses, send_rows):
    own = basis.shape[1]
    width = basis.shape[2]
    frames = latents.shape[0]
    each = latents.shape[1]
    halo = send_rows.shape[1]
    tris = triangles.shape[1]
    hings = hinges.shape[1]
    ext = own + 2 * halo
    half = own // 2
    patches = lax.axis_size("patch")
    total_frames = frames * lax.axis_size("frame")
    chips = patches // 2
    onward = [(i, (i + 1) % patches) for i in range(patches)]
    backward = [((i + 1) % patches, i) for i in range(patches)]
    sibling = [(i, i ^ 1) for i in range(patches)]
    partner = [(0, 1), (1, 0)]
    same_core = [[2 * i + c for i in range(chips)] for c in range(2)]
    core = (lax.axis_index("patch") % 2).astype(jnp.int32).reshape(1)
    half_index = lax.axis_index("frame").astype(jnp.int32).reshape(1)

    sent = ((3 * halo + 16, width), BF)
    [copies] = call(copies_kernel, [((chips, each, frames), BF)], latents.T)
    rows_prev, rows_next = call(
        rows_kernel, [sent, sent], send_rows, basis, rest_pos, room=48
    )
    lat_core = lax.all_to_all(
        copies, "patch", 0, 0, tiled=True, axis_index_groups=same_core
    )
    halo_prv = lax.ppermute(rows_next, "patch", onward)
    halo_nxt = lax.ppermute(rows_prev, "patch", backward)
    d, dt, b, bt, lap, sq, own_t = call(
        own_kernel,
        [
            ((2 * tris, ext), BF),
            ((ext, 2 * tris), BF),
            ((hings, ext), BF),
            ((ext, hings), BF),
            ((ext, ext), BF),
            ((tris, 128), F32),
            ((width, 3 * own), BF),
        ],
        triangles, hinges, rest_sq, basis,
        macs=1 << 30,
    )
    edge, vert, halo_t = call(
        functools.partial(halo_kernel, total_frames),
        [((2 * tris, 128), F32), ((ext, 128), F32), ((width, 6 * halo), BF)],
        rest_pos, masses[None], halo_prv, halo_nxt, bend_rest, d, b, bt,
        macs=1 << 30,
    )
    lat_sib = lax.ppermute(lat_core, "patch", sibling)
    lat_all, f_own, f_prv, f_nxt, keep, give = call(
        functools.partial(elastic_kernel, total_frames, min(frames, 256)),
        [
            ((width, frames), BF),
            ((3 * own, frames), F32),
            ((3 * halo, frames), BF),
            ((3 * halo, frames), BF),
            ((chips, each, frames), BF),
            ((chips, each, frames), BF),
        ],
        core, lat_core, lat_sib, basis, halo_prv, halo_nxt, d, dt, lap, edge, vert, sq,
        own_t, halo_t,
        scalars=1, scratch=[pltpu.VMEM((3 * ext, frames), BF)], macs=5 << 30, room=32,
    )

    back_nxt = lax.ppermute(f_prv, "patch", backward)
    back_prv = lax.ppermute(f_nxt, "patch", onward)

    got = lax.ppermute(give, "patch", sibling)
    [pair] = call(pair_kernel, [((chips, each, frames), BF)], keep, got)
    shares = lax.all_to_all(pair, "patch", 0, 0, tiled=True, axis_index_groups=same_core)
    [latent_grad] = call(share_kernel, [((each, frames), F32)], shares)

    far_core = lax.ppermute(lat_core, "frame", partner)
    far_sib = lax.ppermute(far_core, "patch", sibling)

    piece = ((3 * half, frames), BF)
    mine, other = call(
        adjoint_kernel, [piece, piece], half_index, send_rows, f_own, back_prv, back_nxt,
        scalars=1, macs=10 << 30,
    )
    received = lax.ppermute(other, "frame", partner)
    part, lat_far = call(
        own_part_far_kernel, [((3 * half, width), BF), ((width, frames), BF)],
        core, mine, lat_all, far_core, far_sib, scalars=1, macs=3 * half * width * frames,
    )
    basis_grad = pl.pallas_call(
        last_kernel,
        in_specs=[VMEM, VMEM, VMEM, pl.BlockSpec(memory_space=pltpu.HBM)],
        out_specs=pl.BlockSpec(memory_space=pl.ANY),
        out_shape=jax.ShapeDtypeStruct((3 * half, width), F32),
        scratch_shapes=[pltpu.VMEM((3 * half, width), F32), pltpu.SemaphoreType.DMA((3,))],
        compiler_params=pltpu.CompilerParams(vmem_limit_bytes=24 << 20),
    )(part, received, lat_far, latent_grad)
    return basis_grad.reshape(3, half, width), latent_grad.T


def solution(mesh):
    return jax.shard_map(
        local,
        mesh=mesh,
        in_specs=(
            P(None, "patch", None),
            P("frame", "patch"),
            P(None, "patch"),
            P(None, "patch"),
            P(None, "patch"),
            P(None, "patch"),
            P(None, "patch"),
            P("patch"),
            P(None, "patch"),
        ),
        out_specs=(P(None, ("patch", "frame"), None), P("frame", "patch")),
        check_vma=False,
    )
```

```python
import functools
import math

import jax
import jax.numpy as jnp
from jax import lax
from jax.experimental import pallas as pl
from jax.experimental.pallas import tpu as pltpu
from jax.sharding import PartitionSpec as P

MEMBRANE = 5.0
BENDING = 5.0
GRAVITY = 40.0
BF = jnp.bfloat16
F32 = jnp.float32
NN = (((1,), (0,)), ((), ()))
TN = (((0,), (0,)), ((), ()))
NT = (((1,), (1,)), ((), ()))


def dot(a, b, dims=NN):
    return lax.dot_general(a, b, dims, preferred_element_type=F32)


def exact_dot(a, b):
    total = None
    for _ in range(3):
        part = b.astype(BF)
        b = b - part.astype(F32)
        term = dot(a, part)
        total = term if total is None else total + term
    return total


def one_hot(rows, ids):
    return (lax.broadcasted_iota(jnp.int32, (rows, ids.shape[1]), 0) == ids).astype(F32)


def column_block(rows):
    n, width = rows.shape
    return jnp.concatenate([rows, jnp.zeros((128 - n, width), F32)], axis=0).T


def interleave(core, mine_ref, other_ref, out_ref):
    chips, each, _ = mine_ref.shape
    for i in range(chips):
        out_ref[pl.ds(pl.multiple_of((2 * i + core) * each, each), each), :] = mine_ref[i]
        out_ref[pl.ds(pl.multiple_of((2 * i + 1 - core) * each, each), each), :] = other_ref[i]


def send(ref):
    if isinstance(ref, Stored):
        ref.send()


def copies_kernel(shard_ref, copies_ref):
    for i in range(copies_ref.shape[0]):
        copies_ref[i] = shard_ref[...]


def rows_kernel(send_ref, basis_ref, rest_ref, prev_ref, next_ref):
    own, halo = basis_ref.shape[1], send_ref.shape[1]
    rest = rest_ref[...]
    parts = []
    for _ in range(3):
        part = rest.astype(BF)
        rest = rest - part.astype(F32)
        parts.append(part.astype(F32))
    parts.append(jnp.zeros((7, own), F32))
    parts = jnp.concatenate(parts, axis=0).astype(BF)
    for row, out in ((0, prev_ref), (1, next_ref)):
        sel = one_hot(own, send_ref[row : row + 1, :]).astype(BF)
        for c in range(3):
            out[c * halo : (c + 1) * halo, :] = dot(sel, basis_ref[c], TN).astype(BF)
        out[3 * halo :, :] = jnp.zeros((out.shape[0] - 3 * halo, out.shape[1]), BF)
        out[3 * halo :, :halo] = dot(parts, sel).astype(BF)
        send(out)


def own_kernel(
    tri_ref, hin_ref, sq_ref, own_ref, d_ref, dt_ref, b_ref, bt_ref, lap_ref, sqc_ref, own_t_ref
):
    ext = dt_ref.shape[0]
    own_n = own_ref.shape[1]
    sqc_ref[...] = column_block(sq_ref[...])
    for c in range(3):
        own_t_ref[:, c * own_n : (c + 1) * own_n] = own_ref[c].T
    t = tri_ref.shape[1]
    a, b, c = (one_hot(ext, tri_ref[i : i + 1, :]) for i in range(3))
    for at, part in ((0, b - a), (t, c - b)):
        dt_ref[:, at : at + t] = part.astype(BF)
        d_ref[at : at + t, :] = part.T.astype(BF)
    a, b, c, d = (one_hot(ext, hin_ref[i : i + 1, :]) for i in range(4))
    part = c + d - a - b
    bt_ref[...] = part.astype(BF)
    b_ref[...] = part.T.astype(BF)
    lap_ref[...] = dot(bt_ref[...], b_ref[...]).astype(BF)


def halo_kernel(
    frames,
    rest_ref, mass_ref, prv_ref, nxt_ref, bend_ref, d_ref, b_ref, bt_ref,
    edge_ref, vert_ref, halo_t_ref,
):
    halo = (prv_ref.shape[0] - 16) // 3
    pieces = [jnp.concatenate([rest_ref[...], mass_ref[...]], axis=0)]
    for ref in (prv_ref, nxt_ref):
        tail = ref[3 * halo :, :halo].astype(F32)
        pieces.append(
            jnp.concatenate([tail[0:3] + tail[3:6] + tail[6:9], jnp.zeros((1, halo), F32)], axis=0)
        )
    cols = column_block(jnp.concatenate(pieces, axis=1))
    edge_ref[...] = exact_dot(d_ref[...], cols)
    stretch = exact_dot(b_ref[...], cols) - column_block(bend_ref[...])
    force = exact_dot(bt_ref[...], stretch) * (2.0 * BENDING / frames)
    lane = lax.broadcasted_iota(jnp.int32, cols.shape, 1)
    weight = jnp.sum(jnp.where(lane == 3, cols, 0.0), axis=1, keepdims=True) * (GRAVITY / frames)
    vert_ref[...] = force + jnp.where(lane == 2, weight, 0.0)
    halo_t_ref[:, : 3 * halo] = prv_ref[: 3 * halo, :].T
    halo_t_ref[:, 3 * halo :] = nxt_ref[: 3 * halo, :].T


def elastic_kernel(
    frames, step,
    core_ref, mine_ref, sib_ref, own_ref, prv_ref, nxt_ref, d_ref, dt_ref, lap_ref, edge_ref,
    vert_ref, sq_ref, own_t_ref, halo_t_ref,
    lat_ref, f_own_ref, f_prv_ref, f_nxt_ref, keep_ref, give_ref, f_all_ref,
):
    own_n = own_ref.shape[1]
    t = sq_ref.shape[0]
    halo = f_prv_ref.shape[0] // 3
    interleave(core_ref[0], mine_ref, sib_ref, lat_ref)
    scale = 4.0 * MEMBRANE / frames
    for at in range(0, lat_ref.shape[1], step):
        here = slice(at, at + step)
        lat = lat_ref[:, here]
        x_prv = dot(prv_ref[: 3 * halo, :], lat).astype(BF)
        x_nxt = dot(nxt_ref[: 3 * halo, :], lat).astype(BF)
        points, edges = [], []
        for c in range(3):
            x = jnp.concatenate(
                [
                    dot(own_ref[c], lat).astype(BF),
                    x_prv[c * halo : (c + 1) * halo],
                    x_nxt[c * halo : (c + 1) * halo],
                ],
                axis=0,
            )
            points.append(x)
            edges.append(dot(d_ref[...], x) + edge_ref[:, c : c + 1])
        e1 = [e[:t] for e in edges]
        e2 = [e[t:] for e in edges]
        e3 = [u + v for u, v in zip(e1, e2)]
        s1, s2, s3 = (
            scale * (e[0] * e[0] + e[1] * e[1] + e[2] * e[2] - sq_ref[:, i : i + 1])
            for i, e in enumerate((e1, e2, e3))
        )
        for c in range(3):
            third = s3 * e3[c]
            g = jnp.concatenate(
                [(s1 * e1[c] + third).astype(BF), (s2 * e2[c] + third).astype(BF)], axis=0
            )
            f = dot(dt_ref[...], g) + dot(lap_ref[...], points[c]) * (2.0 * BENDING / frames)
            f = f + vert_ref[:, c : c + 1]
            f_own_ref[c * own_n : (c + 1) * own_n, here] = f[:own_n]
            short = f.astype(BF)
            f_prv_ref[c * halo : (c + 1) * halo, here] = short[own_n : own_n + halo]
            f_nxt_ref[c * halo : (c + 1) * halo, here] = short[own_n + halo :]
            for at_row, size, first in (
                (c * own_n, own_n, 0),
                (3 * own_n + c * halo, halo, own_n),
                (3 * (own_n + halo) + c * halo, halo, own_n + halo),
            ):
                f_all_ref[at_row : at_row + size, here] = short[first : first + size]
    each = mine_ref.shape[1]
    first = core_ref[0] == 0
    for at in range(0, lat_ref.shape[0], 256):
        rows = slice(at, at + 256)
        both = jnp.concatenate([own_t_ref[rows, :], halo_t_ref[rows, :]], axis=1)
        block = dot(both, f_all_ref[...])
        for i in range(0, 256, 2 * each):
            low, high = block[i : i + each], block[i + each : i + 2 * each]
            chip = (at + i) // (2 * each)
            keep_ref[chip] = jnp.where(first, low, high).astype(BF)
            give_ref[chip] = jnp.where(first, high, low).astype(BF)


def pair_kernel(a_ref, b_ref, out_ref):
    out_ref[...] = (a_ref[...].astype(F32) + b_ref[...].astype(F32)).astype(BF)


def share_kernel(shares_ref, out_ref):
    total = shares_ref[0].astype(F32)
    for i in range(1, shares_ref.shape[0]):
        total = total + shares_ref[i].astype(F32)
    out_ref[...] = total


def adjoint_kernel(
    half_ref, send_ref, f_own_ref, back_prv_ref, back_nxt_ref, mine_ref, other_ref
):
    halo = send_ref.shape[1]
    own = f_own_ref.shape[0] // 3
    half = own // 2
    first = half_ref[0] == 0
    to_prev = one_hot(own, send_ref[0:1, :]).astype(BF)
    to_next = one_hot(own, send_ref[1:2, :]).astype(BF)
    for c in range(3):
        rows = slice(c * halo, (c + 1) * halo)
        total = f_own_ref[c * own : (c + 1) * own, :]
        total = total + dot(to_prev, back_prv_ref[rows, :]) + dot(to_next, back_nxt_ref[rows, :])
        low, high = total[:half], total[half:]
        mine_ref[c * half : (c + 1) * half, :] = jnp.where(first, low, high).astype(BF)
        other_ref[c * half : (c + 1) * half, :] = jnp.where(first, high, low).astype(BF)


def own_part_far_kernel(core_ref, mine_ref, lat_ref, core_lat_ref, sib_lat_ref, out_ref, far_lat_ref):
    interleave(core_ref[0], core_lat_ref, sib_lat_ref, far_lat_ref)
    out_ref[...] = dot(mine_ref[...], lat_ref[...], NT).astype(BF)


def last_kernel(part_ref, far_ref, lat_ref, done_ref, out_ref, sum_ref, sem):
    third = out_ref.shape[0] // 3
    copies = []
    for c in range(3):
        rows = slice(c * third, (c + 1) * third)
        far = dot(far_ref[rows, :], lat_ref[...], NT).astype(BF).astype(F32)
        sum_ref[rows, :] = part_ref[rows, :].astype(F32) + far
        copies.append(pltpu.make_async_copy(sum_ref.at[rows], out_ref.at[rows], sem.at[c]))
        copies[-1].start()
    for copy in copies:
        copy.wait()


class Loaded:
    def __init__(self, source, ref, sem):
        self.ref, self.copy = ref, pltpu.make_async_copy(source, ref, sem)
        self.shape, self.waiting = ref.shape, True
        self.copy.start()

    def wait(self):
        if self.waiting:
            self.copy.wait()
            self.waiting = False

    def __getitem__(self, index):
        self.wait()
        return self.ref[index]


class Stored:
    def __init__(self, ref, target, sem):
        self.ref, self.copy = ref, pltpu.make_async_copy(ref, target, sem)
        self.shape, self.open = ref.shape, True

    def __setitem__(self, index, value):
        self.ref[index] = value

    def __getitem__(self, index):
        return self.ref[index]

    def send(self):
        if self.open:
            self.copy.start()
            self.open = False


SMEM = pl.BlockSpec(memory_space=pltpu.SMEM)
ANY = pl.BlockSpec(memory_space=pl.ANY)
VMEM = pl.BlockSpec(memory_space=pltpu.VMEM)


def call(kernel, outs, *args, scalars=0, direct=True, near=(), scratch=(), macs=0, room=0):
    moved = sum(a.size * a.dtype.itemsize for a in args)
    moved += sum(math.prod(s) * jnp.dtype(d).itemsize for s, d in outs)
    ins, n_in, n_out = args[scalars:], len(args) - scalars, len(outs)
    params = pltpu.CompilerParams(vmem_limit_bytes=(room or 24) << 20)
    if direct:
        return pl.pallas_call(
            kernel,
            cost_estimate=pl.CostEstimate(flops=2 * macs, bytes_accessed=moved, transcendentals=0),
            in_specs=[SMEM] * scalars + [VMEM] * n_in,
            out_specs=[VMEM] * n_out,
            out_shape=[jax.ShapeDtypeStruct(s, d) for s, d in outs],
            scratch_shapes=list(scratch),
            compiler_params=params,
        )(*args)
    far = [i for i in range(n_in) if i + scalars not in near]
    n_far = len(far)

    def body(*refs):
        numbers, refs = refs[:scalars], refs[scalars:]
        sources, targets, refs = refs[:n_in], refs[n_in : n_in + n_out], refs[n_in + n_out :]
        held, made, refs = refs[:n_far], refs[n_far : n_far + n_out], refs[n_far + n_out :]
        in_sem, out_sem, *rest = refs
        loads = list(sources)
        for i, at in enumerate(far):
            loads[at] = Loaded(sources[at], held[i], in_sem.at[i])
        stores = [Stored(v, x, out_sem.at[i]) for i, (x, v) in enumerate(zip(targets, made))]
        kernel(*numbers, *loads, *stores, *rest)
        for at in far:
            loads[at].wait()
        for store in stores:
            store.send()
        for store in stores:
            store.copy.wait()

    return pl.pallas_call(
        body,
        cost_estimate=pl.CostEstimate(flops=2 * macs, bytes_accessed=moved, transcendentals=0),
        in_specs=[SMEM] * scalars + [ANY if i in far else VMEM for i in range(n_in)],
        out_specs=[ANY] * n_out,
        out_shape=[jax.ShapeDtypeStruct(s, d) for s, d in outs],
        scratch_shapes=[pltpu.VMEM(ins[i].shape, ins[i].dtype) for i in far]
        + [pltpu.VMEM(s, d) for s, d in outs]
        + [pltpu.SemaphoreType.DMA((max(n_far, 1),)), pltpu.SemaphoreType.DMA((n_out,))]
        + list(scratch),
        compiler_params=params,
    )(*args)


def local(basis, latents, rest_pos, triangles, hinges, rest_sq, bend_rest, masses, send_rows):
    own = basis.shape[1]
    width = basis.shape[2]
    frames = latents.shape[0]
    each = latents.shape[1]
    halo = send_rows.shape[1]
    tris = triangles.shape[1]
    hings = hinges.shape[1]
    ext = own + 2 * halo
    half = own // 2
    patches = lax.axis_size("patch")
    total_frames = frames * lax.axis_size("frame")
    chips = patches // 2
    onward = [(i, (i + 1) % patches) for i in range(patches)]
    backward = [((i + 1) % patches, i) for i in range(patches)]
    sibling = [(i, i ^ 1) for i in range(patches)]
    partner = [(0, 1), (1, 0)]
    same_core = [[2 * i + c for i in range(chips)] for c in range(2)]
    core = (lax.axis_index("patch") % 2).astype(jnp.int32).reshape(1)
    half_index = lax.axis_index("frame").astype(jnp.int32).reshape(1)

    sent = ((3 * halo + 16, width), BF)
    [copies] = call(copies_kernel, [((chips, each, frames), BF)], latents.T)
    rows_prev, rows_next = call(
        rows_kernel, [sent, sent], send_rows, basis, rest_pos, direct=False, room=60
    )
    lat_core = lax.all_to_all(
        copies, "patch", 0, 0, tiled=True, axis_index_groups=same_core
    )
    halo_prv = lax.ppermute(rows_next, "patch", onward)
    halo_nxt = lax.ppermute(rows_prev, "patch", backward)
    d, dt, b, bt, lap, sq, own_t = call(
        own_kernel,
        [
            ((2 * tris, ext), BF),
            ((ext, 2 * tris), BF),
            ((hings, ext), BF),
            ((ext, hings), BF),
            ((ext, ext), BF),
            ((tris, 128), F32),
            ((width, 3 * own), BF),
        ],
        triangles, hinges, rest_sq, basis,
        macs=1 << 30,
    )
    edge, vert, halo_t = call(
        functools.partial(halo_kernel, total_frames),
        [((2 * tris, 128), F32), ((ext, 128), F32), ((width, 6 * halo), BF)],
        rest_pos, masses[None], halo_prv, halo_nxt, bend_rest, d, b, bt,
        macs=1 << 30,
    )
    lat_sib = lax.ppermute(lat_core, "patch", sibling)
    lat_all, f_own, f_prv, f_nxt, keep, give = call(
        functools.partial(elastic_kernel, total_frames, min(frames, 256)),
        [
            ((width, frames), BF),
            ((3 * own, frames), F32),
            ((3 * halo, frames), BF),
            ((3 * halo, frames), BF),
            ((chips, each, frames), BF),
            ((chips, each, frames), BF),
        ],
        core, lat_core, lat_sib, basis, halo_prv, halo_nxt, d, dt, lap, edge, vert, sq,
        own_t, halo_t,
        scalars=1, scratch=[pltpu.VMEM((3 * ext, frames), BF)], macs=5 << 30, room=32,
    )

    back_nxt = lax.ppermute(f_prv, "patch", backward)
    back_prv = lax.ppermute(f_nxt, "patch", onward)

    got = lax.ppermute(give, "patch", sibling)
    [pair] = call(pair_kernel, [((chips, each, frames), BF)], keep, got)
    shares = lax.all_to_all(pair, "patch", 0, 0, tiled=True, axis_index_groups=same_core)
    [latent_grad] = call(share_kernel, [((each, frames), F32)], shares)

    far_core = lax.ppermute(lat_core, "frame", partner)
    far_sib = lax.ppermute(far_core, "patch", sibling)

    piece = ((3 * half, frames), BF)
    mine, other = call(
        adjoint_kernel, [piece, piece], half_index, send_rows, f_own, back_prv, back_nxt,
        scalars=1, macs=10 << 30,
    )
    received = lax.ppermute(other, "frame", partner)
    part, lat_far = call(
        own_part_far_kernel, [((3 * half, width), BF), ((width, frames), BF)],
        core, mine, lat_all, far_core, far_sib, scalars=1, macs=3 * half * width * frames,
    )
    basis_grad = pl.pallas_call(
        last_kernel,
        in_specs=[VMEM, VMEM, VMEM, ANY],
        out_specs=ANY,
        out_shape=jax.ShapeDtypeStruct((3 * half, width), F32),
        scratch_shapes=[pltpu.VMEM((3 * half, width), F32), pltpu.SemaphoreType.DMA((3,))],
        compiler_params=pltpu.CompilerParams(vmem_limit_bytes=24 << 20),
    )(part, received, lat_far, latent_grad)
    return basis_grad.reshape(3, half, width), latent_grad.T


def solution(mesh):
    return jax.shard_map(
        local,
        mesh=mesh,
        in_specs=(
            P(None, "patch", None),
            P("frame", "patch"),
            P(None, "patch"),
            P(None, "patch"),
            P(None, "patch"),
            P(None, "patch"),
            P(None, "patch"),
            P("patch"),
            P(None, "patch"),
        ),
        out_specs=(P(None, ("patch", "frame"), None), P("frame", "patch")),
        check_vma=False,
    )
```

```python
import functools
import math

import jax
import jax.numpy as jnp
from jax import lax
from jax.experimental import pallas as pl
from jax.experimental.pallas import tpu as pltpu
from jax.sharding import PartitionSpec as P

MEMBRANE = 5.0
BENDING = 5.0
GRAVITY = 40.0
BF = jnp.bfloat16
F32 = jnp.float32
NN = (((1,), (0,)), ((), ()))
TN = (((0,), (0,)), ((), ()))
NT = (((1,), (1,)), ((), ()))


def dot(a, b, dims=NN):
    return lax.dot_general(a, b, dims, preferred_element_type=F32)


def exact_dot(a, b):
    total = None
    for _ in range(3):
        part = b.astype(BF)
        b = b - part.astype(F32)
        term = dot(a, part)
        total = term if total is None else total + term
    return total


def one_hot(rows, ids):
    return (lax.broadcasted_iota(jnp.int32, (rows, ids.shape[1]), 0) == ids).astype(F32)


def column_block(rows):
    n, width = rows.shape
    return jnp.concatenate([rows, jnp.zeros((128 - n, width), F32)], axis=0).T


def interleave(core, mine_ref, other_ref, out_ref):
    chips, each, _ = mine_ref.shape
    for i in range(chips):
        out_ref[pl.ds(pl.multiple_of((2 * i + core) * each, each), each), :] = mine_ref[i]
        out_ref[pl.ds(pl.multiple_of((2 * i + 1 - core) * each, each), each), :] = other_ref[i]


def send(ref):
    if isinstance(ref, Stored):
        ref.send()


def copies_kernel(shard_ref, copies_ref):
    for i in range(copies_ref.shape[0]):
        copies_ref[i] = shard_ref[...]


def rows_kernel(send_ref, basis_ref, rest_ref, prev_ref, next_ref):
    own, halo = basis_ref.shape[1], send_ref.shape[1]
    rest = rest_ref[...]
    parts = []
    for _ in range(3):
        part = rest.astype(BF)
        rest = rest - part.astype(F32)
        parts.append(part.astype(F32))
    parts.append(jnp.zeros((7, own), F32))
    parts = jnp.concatenate(parts, axis=0).astype(BF)
    for row, out in ((0, prev_ref), (1, next_ref)):
        sel = one_hot(own, send_ref[row : row + 1, :]).astype(BF)
        for c in range(3):
            out[c * halo : (c + 1) * halo, :] = dot(sel, basis_ref[c], TN).astype(BF)
        out[3 * halo :, :] = jnp.zeros((out.shape[0] - 3 * halo, out.shape[1]), BF)
        out[3 * halo :, :halo] = dot(parts, sel).astype(BF)
        send(out)


def own_kernel(
    tri_ref, hin_ref, sq_ref, own_ref, d_ref, dt_ref, b_ref, bt_ref, lap_ref, sqc_ref, own_t_ref
):
    ext = dt_ref.shape[0]
    own_n = own_ref.shape[1]
    sqc_ref[...] = column_block(sq_ref[...])
    for c in range(3):
        own_t_ref[:, c * own_n : (c + 1) * own_n] = own_ref[c].T
    t = tri_ref.shape[1]
    a, b, c = (one_hot(ext, tri_ref[i : i + 1, :]) for i in range(3))
    for at, part in ((0, b - a), (t, c - b)):
        dt_ref[:, at : at + t] = part.astype(BF)
        d_ref[at : at + t, :] = part.T.astype(BF)
    a, b, c, d = (one_hot(ext, hin_ref[i : i + 1, :]) for i in range(4))
    part = c + d - a - b
    bt_ref[...] = part.astype(BF)
    b_ref[...] = part.T.astype(BF)
    lap_ref[...] = dot(bt_ref[...], b_ref[...]).astype(BF)


def halo_kernel(
    frames,
    rest_ref, mass_ref, prv_ref, nxt_ref, bend_ref, d_ref, b_ref, bt_ref,
    edge_ref, vert_ref, halo_t_ref,
):
    halo = (prv_ref.shape[0] - 16) // 3
    pieces = [jnp.concatenate([rest_ref[...], mass_ref[...]], axis=0)]
    for ref in (prv_ref, nxt_ref):
        tail = ref[3 * halo :, :halo].astype(F32)
        pieces.append(
            jnp.concatenate([tail[0:3] + tail[3:6] + tail[6:9], jnp.zeros((1, halo), F32)], axis=0)
        )
    cols = column_block(jnp.concatenate(pieces, axis=1))
    edge_ref[...] = exact_dot(d_ref[...], cols)
    stretch = exact_dot(b_ref[...], cols) - column_block(bend_ref[...])
    force = exact_dot(bt_ref[...], stretch) * (2.0 * BENDING / frames)
    lane = lax.broadcasted_iota(jnp.int32, cols.shape, 1)
    weight = jnp.sum(jnp.where(lane == 3, cols, 0.0), axis=1, keepdims=True) * (GRAVITY / frames)
    vert_ref[...] = force + jnp.where(lane == 2, weight, 0.0)
    halo_t_ref[:, : 3 * halo] = prv_ref[: 3 * halo, :].T
    halo_t_ref[:, 3 * halo :] = nxt_ref[: 3 * halo, :].T


def elastic_kernel(
    frames, step,
    core_ref, mine_ref, sib_ref, own_ref, prv_ref, nxt_ref, d_ref, dt_ref, lap_ref, edge_ref,
    vert_ref, sq_ref, own_t_ref, halo_t_ref,
    lat_ref, f_own_ref, f_prv_ref, f_nxt_ref, keep_ref, give_ref, f_all_ref,
):
    own_n = own_ref.shape[1]
    t = sq_ref.shape[0]
    halo = f_prv_ref.shape[0] // 3
    interleave(core_ref[0], mine_ref, sib_ref, lat_ref)
    scale = 4.0 * MEMBRANE / frames
    for at in range(0, lat_ref.shape[1], step):
        here = slice(at, at + step)
        lat = lat_ref[:, here]
        x_prv = dot(prv_ref[: 3 * halo, :], lat).astype(BF)
        x_nxt = dot(nxt_ref[: 3 * halo, :], lat).astype(BF)
        points, edges = [], []
        for c in range(3):
            x = jnp.concatenate(
                [
                    dot(own_ref[c], lat).astype(BF),
                    x_prv[c * halo : (c + 1) * halo],
                    x_nxt[c * halo : (c + 1) * halo],
                ],
                axis=0,
            )
            points.append(x)
            edges.append(dot(d_ref[...], x) + edge_ref[:, c : c + 1])
        e1 = [e[:t] for e in edges]
        e2 = [e[t:] for e in edges]
        e3 = [u + v for u, v in zip(e1, e2)]
        s1, s2, s3 = (
            scale * (e[0] * e[0] + e[1] * e[1] + e[2] * e[2] - sq_ref[:, i : i + 1])
            for i, e in enumerate((e1, e2, e3))
        )
        for c in range(3):
            third = s3 * e3[c]
            g = jnp.concatenate(
                [(s1 * e1[c] + third).astype(BF), (s2 * e2[c] + third).astype(BF)], axis=0
            )
            f = dot(dt_ref[...], g) + dot(lap_ref[...], points[c]) * (2.0 * BENDING / frames)
            f = f + vert_ref[:, c : c + 1]
            f_own_ref[c * own_n : (c + 1) * own_n, here] = f[:own_n]
            short = f.astype(BF)
            f_prv_ref[c * halo : (c + 1) * halo, here] = short[own_n : own_n + halo]
            f_nxt_ref[c * halo : (c + 1) * halo, here] = short[own_n + halo :]
            for at_row, size, first in (
                (c * own_n, own_n, 0),
                (3 * own_n + c * halo, halo, own_n),
                (3 * (own_n + halo) + c * halo, halo, own_n + halo),
            ):
                f_all_ref[at_row : at_row + size, here] = short[first : first + size]
    each = mine_ref.shape[1]
    first = core_ref[0] == 0
    for at in range(0, lat_ref.shape[0], 256):
        rows = slice(at, at + 256)
        both = jnp.concatenate([own_t_ref[rows, :], halo_t_ref[rows, :]], axis=1)
        block = dot(both, f_all_ref[...])
        for i in range(0, 256, 2 * each):
            low, high = block[i : i + each], block[i + each : i + 2 * each]
            chip = (at + i) // (2 * each)
            keep_ref[chip] = jnp.where(first, low, high).astype(BF)
            give_ref[chip] = jnp.where(first, high, low).astype(BF)


def pair_kernel(a_ref, b_ref, out_ref):
    out_ref[...] = (a_ref[...].astype(F32) + b_ref[...].astype(F32)).astype(BF)


def share_kernel(shares_ref, out_ref):
    total = shares_ref[0].astype(F32)
    for i in range(1, shares_ref.shape[0]):
        total = total + shares_ref[i].astype(F32)
    out_ref[...] = total


def adjoint_kernel(
    half_ref, send_ref, f_own_ref, back_prv_ref, back_nxt_ref, mine_ref, other_ref
):
    halo = send_ref.shape[1]
    own = f_own_ref.shape[0] // 3
    half = own // 2
    first = half_ref[0] == 0
    to_prev = one_hot(own, send_ref[0:1, :]).astype(BF)
    to_next = one_hot(own, send_ref[1:2, :]).astype(BF)
    for c in range(3):
        rows = slice(c * halo, (c + 1) * halo)
        total = f_own_ref[c * own : (c + 1) * own, :]
        total = total + dot(to_prev, back_prv_ref[rows, :]) + dot(to_next, back_nxt_ref[rows, :])
        low, high = total[:half], total[half:]
        mine_ref[c * half : (c + 1) * half, :] = jnp.where(first, low, high).astype(BF)
        other_ref[c * half : (c + 1) * half, :] = jnp.where(first, high, low).astype(BF)


def own_part_far_kernel(core_ref, mine_ref, lat_ref, core_lat_ref, sib_lat_ref, out_ref, far_lat_ref):
    interleave(core_ref[0], core_lat_ref, sib_lat_ref, far_lat_ref)
    out_ref[...] = dot(mine_ref[...], lat_ref[...], NT).astype(BF)


def last_kernel(part_ref, far_ref, lat_ref, done_ref, out_ref, sum_ref, sem):
    third = out_ref.shape[0] // 3
    copies = []
    for c in range(3):
        rows = slice(c * third, (c + 1) * third)
        far = dot(far_ref[rows, :], lat_ref[...], NT).astype(BF).astype(F32)
        sum_ref[rows, :] = part_ref[rows, :].astype(F32) + far
        copies.append(pltpu.make_async_copy(sum_ref.at[rows], out_ref.at[rows], sem.at[c]))
        copies[-1].start()
    for copy in copies:
        copy.wait()


class Loaded:
    def __init__(self, source, ref, sem):
        self.ref, self.copy = ref, pltpu.make_async_copy(source, ref, sem)
        self.shape, self.waiting = ref.shape, True
        self.copy.start()

    def wait(self):
        if self.waiting:
            self.copy.wait()
            self.waiting = False

    def __getitem__(self, index):
        self.wait()
        return self.ref[index]


class Stored:
    def __init__(self, ref, target, sem):
        self.ref, self.copy = ref, pltpu.make_async_copy(ref, target, sem)
        self.shape, self.open = ref.shape, True

    def __setitem__(self, index, value):
        self.ref[index] = value

    def __getitem__(self, index):
        return self.ref[index]

    def send(self):
        if self.open:
            self.copy.start()
            self.open = False


SMEM = pl.BlockSpec(memory_space=pltpu.SMEM)
ANY = pl.BlockSpec(memory_space=pl.ANY)
VMEM = pl.BlockSpec(memory_space=pltpu.VMEM)


def call(kernel, outs, *args, scalars=0, direct=True, near=(), scratch=(), macs=0, room=0):
    moved = sum(a.size * a.dtype.itemsize for a in args)
    moved += sum(math.prod(s) * jnp.dtype(d).itemsize for s, d in outs)
    ins, n_in, n_out = args[scalars:], len(args) - scalars, len(outs)
    params = pltpu.CompilerParams(vmem_limit_bytes=(room or 24) << 20)
    if direct:
        return pl.pallas_call(
            kernel,
            cost_estimate=pl.CostEstimate(flops=2 * macs, bytes_accessed=moved, transcendentals=0),
            in_specs=[SMEM] * scalars + [VMEM] * n_in,
            out_specs=[VMEM] * n_out,
            out_shape=[jax.ShapeDtypeStruct(s, d) for s, d in outs],
            scratch_shapes=list(scratch),
            compiler_params=params,
        )(*args)
    far = [i for i in range(n_in) if i + scalars not in near]
    n_far = len(far)

    def body(*refs):
        numbers, refs = refs[:scalars], refs[scalars:]
        sources, targets, refs = refs[:n_in], refs[n_in : n_in + n_out], refs[n_in + n_out :]
        held, made, refs = refs[:n_far], refs[n_far : n_far + n_out], refs[n_far + n_out :]
        in_sem, out_sem, *rest = refs
        loads = list(sources)
        for i, at in enumerate(far):
            loads[at] = Loaded(sources[at], held[i], in_sem.at[i])
        stores = [Stored(v, x, out_sem.at[i]) for i, (x, v) in enumerate(zip(targets, made))]
        kernel(*numbers, *loads, *stores, *rest)
        for at in far:
            loads[at].wait()
        for store in stores:
            store.send()
        for store in stores:
            store.copy.wait()

    return pl.pallas_call(
        body,
        cost_estimate=pl.CostEstimate(flops=2 * macs, bytes_accessed=moved, transcendentals=0),
        in_specs=[SMEM] * scalars + [ANY if i in far else VMEM for i in range(n_in)],
        out_specs=[ANY] * n_out,
        out_shape=[jax.ShapeDtypeStruct(s, d) for s, d in outs],
        scratch_shapes=[pltpu.VMEM(ins[i].shape, ins[i].dtype) for i in far]
        + [pltpu.VMEM(s, d) for s, d in outs]
        + [pltpu.SemaphoreType.DMA((max(n_far, 1),)), pltpu.SemaphoreType.DMA((n_out,))]
        + list(scratch),
        compiler_params=params,
    )(*args)


def local(basis, latents, rest_pos, triangles, hinges, rest_sq, bend_rest, masses, send_rows):
    own = basis.shape[1]
    width = basis.shape[2]
    frames = latents.shape[0]
    each = latents.shape[1]
    halo = send_rows.shape[1]
    tris = triangles.shape[1]
    hings = hinges.shape[1]
    ext = own + 2 * halo
    half = own // 2
    patches = lax.axis_size("patch")
    total_frames = frames * lax.axis_size("frame")
    chips = patches // 2
    onward = [(i, (i + 1) % patches) for i in range(patches)]
    backward = [((i + 1) % patches, i) for i in range(patches)]
    sibling = [(i, i ^ 1) for i in range(patches)]
    partner = [(0, 1), (1, 0)]
    same_core = [[2 * i + c for i in range(chips)] for c in range(2)]
    core = (lax.axis_index("patch") % 2).astype(jnp.int32).reshape(1)
    half_index = lax.axis_index("frame").astype(jnp.int32).reshape(1)

    sent = ((3 * halo + 16, width), BF)
    [copies] = call(copies_kernel, [((chips, each, frames), BF)], latents.T)
    rows_prev, rows_next = call(
        rows_kernel, [sent, sent], send_rows, basis, rest_pos, direct=False, room=60
    )
    lat_core = lax.all_to_all(
        copies, "patch", 0, 0, tiled=True, axis_index_groups=same_core
    )
    halo_prv = lax.ppermute(rows_next, "patch", onward)
    halo_nxt = lax.ppermute(rows_prev, "patch", backward)
    d, dt, b, bt, lap, sq, own_t = call(
        own_kernel,
        [
            ((2 * tris, ext), BF),
            ((ext, 2 * tris), BF),
            ((hings, ext), BF),
            ((ext, hings), BF),
            ((ext, ext), BF),
            ((tris, 128), F32),
            ((width, 3 * own), BF),
        ],
        triangles, hinges, rest_sq, basis,
        macs=1 << 30,
    )
    edge, vert, halo_t = call(
        functools.partial(halo_kernel, total_frames),
        [((2 * tris, 128), F32), ((ext, 128), F32), ((width, 6 * halo), BF)],
        rest_pos, masses[None], halo_prv, halo_nxt, bend_rest, d, b, bt,
        macs=1 << 30,
    )
    lat_sib = lax.ppermute(lat_core, "patch", sibling)
    lat_all, f_own, f_prv, f_nxt, keep, give = call(
        functools.partial(elastic_kernel, total_frames, min(frames, 256)),
        [
            ((width, frames), BF),
            ((3 * own, frames), F32),
            ((3 * halo, frames), BF),
            ((3 * halo, frames), BF),
            ((chips, each, frames), BF),
            ((chips, each, frames), BF),
        ],
        core, lat_core, lat_sib, basis, halo_prv, halo_nxt, d, dt, lap, edge, vert, sq,
        own_t, halo_t,
        scalars=1, scratch=[pltpu.VMEM((3 * ext, frames), BF)], macs=5 << 30, room=32,
    )

    back_nxt = lax.ppermute(f_prv, "patch", backward)
    back_prv = lax.ppermute(f_nxt, "patch", onward)

    got = lax.ppermute(give, "patch", sibling)
    [pair] = call(pair_kernel, [((chips, each, frames), BF)], keep, got)
    shares = lax.all_to_all(pair, "patch", 0, 0, tiled=True, axis_index_groups=same_core)
    [latent_grad] = call(share_kernel, [((each, frames), F32)], shares)

    far_core = lax.ppermute(lat_core, "frame", partner)
    far_sib = lax.ppermute(far_core, "patch", sibling)

    piece = ((3 * half, frames), BF)
    mine, other = call(
        adjoint_kernel, [piece, piece], half_index, send_rows, f_own, back_prv, back_nxt,
        scalars=1, direct=False, near=(3, 4), room=60, macs=10 << 30,
    )
    received = lax.ppermute(other, "frame", partner)
    part, lat_far = call(
        own_part_far_kernel, [((3 * half, width), BF), ((width, frames), BF)],
        core, mine, lat_all, far_core, far_sib, scalars=1, macs=3 * half * width * frames,
    )
    basis_grad = pl.pallas_call(
        last_kernel,
        in_specs=[VMEM, VMEM, VMEM, ANY],
        out_specs=ANY,
        out_shape=jax.ShapeDtypeStruct((3 * half, width), F32),
        scratch_shapes=[pltpu.VMEM((3 * half, width), F32), pltpu.SemaphoreType.DMA((3,))],
        compiler_params=pltpu.CompilerParams(vmem_limit_bytes=24 << 20),
    )(part, received, lat_far, latent_grad)
    return basis_grad.reshape(3, half, width), latent_grad.T


def solution(mesh):
    return jax.shard_map(
        local,
        mesh=mesh,
        in_specs=(
            P(None, "patch", None),
            P("frame", "patch"),
            P(None, "patch"),
            P(None, "patch"),
            P(None, "patch"),
            P(None, "patch"),
            P(None, "patch"),
            P("patch"),
            P(None, "patch"),
        ),
        out_specs=(P(None, ("patch", "frame"), None), P("frame", "patch")),
        check_vma=False,
    )
```
